32 devices in a mesh: section: 4 (over y, x), expert: 8 (over z, core).
Axes of the slice: x: 2, y: 2, z: 4, core: 2. Of those that a mesh axis runs over, the one named last changes fastest.
Arguments:
- upstream_dy: bfloat16 [4, 2, 512, 6144], P('section', None, 'expert'), may hold values from -6 to 6
- gate_logits: float32 [4, 2, 512, 2], P('section', None, 'expert'), may hold values from -8 to 8
- expert_ids: int32 [4, 2, 512, 2], P('section', None, 'expert'), may hold values from 0 to 3, all different within a row; in each aligned block of 64 rows (0 to 63, 64 to 127, ..., all dimensions but the last counted through in order) at most 36 rows name the same one
- saved_hidden: bfloat16 [4, 2, 8, 36, 32768], P('section', None, None, None, 'expert'), may hold values from -6 to 6
- down_weight: bfloat16 [4, 32768, 6144], P('section', 'expert'), may hold values from -0.0625 to 0.0625
- router_weight: float32 [4, 6144, 4], P('section'), may hold values from -0.078125 to 0.078125
Outputs:
- hidden_grad: bfloat16 [4, 2, 8, 36, 32768], P('section', None, None, None, 'expert')
- upstream_grad: bfloat16 [4, 2, 512, 6144], P('section', None, 'expert')
The draws below stay inside these ranges and needn't reach their ends.
Inputs may be any that keep to these rules, and one draw needn't show every extreme that they name: `expert_ids`: the two experts of a token differ. In each device's block of 64 tokens of one microbatch no expert is named by more than 36 tokens, a bound that some block reaches.
All inputs are finite; a program needn't handle non-finite values.
Results may differ from the reference program's by a relative error of at most 0.0045.
Values may be sent and summed in bfloat16 or wider, within the bound.
No kernel may reach another device: no remote copies, remote signals or barrier semaphores. Data moves between devices by JAX's collectives and lax.ppermute only.
A program may use at most 192 MiB of HBM per device.

```python
import math
import jax
import jax.numpy as jnp
import numpy as np
from jax import lax

D = 6144
FF_WIN = 8192
EXPERTS = 4
MICRO = 2
TOK_MB = 64
CAP = 36
SECTIONS = 4
SOURCES = 8
TOKENS = 512


def levels(stream_key, dims, split, smallest, largest):
    gain, own = 1.0, jax.random.fold_in(stream_key, 6)
    for position, parts in split:
        draws = jnp.exp(jax.random.uniform(jax.random.fold_in(own, position), (parts,), jnp.float32, smallest / len(split), largest / len(split)))
        gain = gain * jnp.repeat(draws, dims[position] // parts).reshape([-1 if axis == position else 1 for axis in range(len(dims))])
    return gain


def assign_block(own_key, own, number, rows, number_of, top, bound, skew):
    ranking = jax.random.permutation(own_key, number_of)
    heavy_load, ordinary = load_shares(number_of, rows * top, bound, skew, True), load_shares(number_of, rows * top, bound, skew, False)
    places = jnp.arange(number_of)

    def named(lengths, rotation):
        used = int((lengths > 0).sum())
        fixed = max(1, used // 4)
        moved = fixed + (places - fixed + rotation * (used - fixed)) % max(1, number_of - fixed)
        return jnp.zeros((number_of,), jnp.int32).at[ranking[jnp.where(places < fixed, places, moved)]].set(jnp.asarray(lengths, jnp.int32))

    lengths = jnp.where(number % 4 == 0, named(heavy_load, number // 4), named(ordinary, number - number // 4 - 1))
    mixed = jax.random.permutation(jax.random.fold_in(own, 3), number_of)
    giver, taker = mixed[0:number_of // 2 * 2:2], mixed[1:number_of // 2 * 2:2]
    margin = jnp.minimum(lengths[giver] - 1, bound - lengths[taker]) // 2
    margin = jnp.where((giver == ranking[0]) | (taker == ranking[0]) | (lengths[taker] == 0), 0, jnp.maximum(margin, 0))
    moved = jax.random.randint(jax.random.fold_in(own, 4), (number_of // 2,), 0, 1 << 20) % (margin + 1)
    lengths = lengths.at[giver].add(-moved).at[taker].add(moved)
    members = jnp.searchsorted(jnp.cumsum(lengths), jnp.arange(rows * top), side="right").astype(jnp.int32)
    grid = members.reshape(top, rows).T
    grid = grid[jax.random.permutation(jax.random.fold_in(own, 1), rows)]
    rotation = jax.random.randint(jax.random.fold_in(own, 2), (rows, 1), 0, top)
    return jnp.take_along_axis(grid, (jnp.arange(top)[None, :] + rotation) % top, axis=1)


def load_shares(amount, total, reach, skew, full):
    portions = [(1 << 20) // math.isqrt(rank ** skew) + 1 for rank in range(1, amount + 1)]
    largest = reach if full else min(reach, max(-(-total // amount), total * portions[0] // sum(portions)))
    least = 1 if total - largest >= amount - 1 else 0
    counts, surplus = [largest] + [least] * (amount - 1), total - largest - least * (amount - 1)
    while surplus > 0:
        free = [i for i in range(1, amount) if counts[i] < largest] or [i for i in range(1, amount) if counts[i] < reach]
        whole, remaining = sum([portions[i] for i in free]), surplus
        for i in free:
            addition = min(reach - counts[i], max(1, remaining * portions[i] // whole), surplus)
            counts[i] = counts[i] + addition
            surplus = surplus - addition
    return np.array(counts)


def centred(own_key, dims, width, most, cuts=(), kind=jnp.bfloat16):
    array = width * jax.random.normal(own_key, dims, jnp.float32)
    if cuts:
        array = array * levels(own_key, dims, cuts, -0.22, 0.18)
    return jnp.clip(array, -most, most).astype(kind)


def setup_inputs(seed: int = 0) -> dict:
    splits = jax.random.split(jax.random.key(seed), 7)
    upstream_dy = centred(splits[0], (SECTIONS, MICRO, TOKENS, D), 1.0, 6.0, ((0, 4), (2, 8)))
    gate_logits = centred(splits[1], (SECTIONS, MICRO, TOKENS, 2), 1.5, 8.0, ((0, 4), (2, 8)), jnp.float32)
    expert_ids_keys = jax.random.split(jax.random.fold_in(splits[2], 1), SECTIONS * MICRO * TOKENS // TOK_MB)
    expert_ids_turns = jax.random.permutation(jax.random.fold_in(splits[2], 3), SECTIONS * MICRO * TOKENS // TOK_MB)
    expert_ids = jax.vmap(lambda own, number: assign_block(jax.random.fold_in(splits[2], 2), own, number, TOK_MB, EXPERTS, 2, CAP, 1))(expert_ids_keys, expert_ids_turns).reshape((SECTIONS, MICRO, TOKENS, 2))
    saved_hidden = centred(splits[3], (SECTIONS, MICRO, SOURCES, CAP, EXPERTS * FF_WIN), 1.0, 6.0, ((0, 4), (4, 8)))
    down_weight = centred(splits[4], (SECTIONS, EXPERTS * FF_WIN, D), FF_WIN ** -0.5, 0.0625, ((0, 4), (1, 8)))
    router_weight = centred(splits[5], (SECTIONS, D, EXPERTS), D ** -0.5, 0.078125, ((0, 4),), jnp.float32)
    return {"upstream_dy": upstream_dy, "gate_logits": gate_logits, "expert_ids": expert_ids, "saved_hidden": saved_hidden, "down_weight": down_weight, "router_weight": router_weight}


def reference(upstream_dy, gate_logits, expert_ids, saved_hidden, down_weight, router_weight):
    highest = lax.Precision.HIGHEST
    expert_range = jnp.arange(EXPERTS, dtype=jnp.int32)
    slot_index = jnp.arange(CAP).astype(jnp.float32)
    section_grads = []
    section_inputs = []
    for section_id in range(SECTIONS):
        micro_grads = []
        micro_inputs = []
        for micro_id in range(MICRO):
            out_grad = upstream_dy[section_id, micro_id]
            logits = gate_logits[section_id, micro_id]
            gate_prob = jax.nn.sigmoid(logits - logits[:, ::-1])
            onehot = (expert_ids[section_id, micro_id][:, :, None] == expert_range).astype(jnp.float32)
            picked = jnp.sum(onehot, axis=1).reshape(SOURCES, TOK_MB, EXPERTS)
            slot_rank = jnp.cumsum(picked, axis=1) - picked
            select = picked[:, None] * (slot_rank[:, None] == slot_index[None, :, None, None]).astype(jnp.float32)
            copies = jnp.einsum("scte,std->escd", select, out_grad.astype(jnp.float32).reshape(SOURCES, TOK_MB, D), precision=highest).astype(jnp.bfloat16)
            gate_expert = jnp.sum(onehot * gate_prob[:, :, None], axis=1).reshape(SOURCES, TOK_MB, EXPERTS)
            slot_gate = jnp.einsum("scte,ste->esc", select, gate_expert, precision=highest).astype(jnp.bfloat16)
            slot_gate = lax.optimization_barrier(slot_gate).astype(jnp.float32)
            grads_list = []
            partial_list = []
            for expert_id in range(EXPERTS):
                weight = down_weight[section_id, expert_id * FF_WIN:(expert_id + 1) * FF_WIN]
                hidden_raw = jnp.dot(copies[expert_id].reshape(SOURCES * CAP, D), weight.T, preferred_element_type=jnp.float32).reshape(SOURCES, CAP, FF_WIN)
                grads_list.append((slot_gate[expert_id][:, :, None] * hidden_raw).astype(jnp.bfloat16))
                saved = saved_hidden[section_id, micro_id, :, :, expert_id * FF_WIN:(expert_id + 1) * FF_WIN].astype(jnp.float32)
                partial_list.append(jnp.sum(hidden_raw * saved, axis=-1))
            micro_grads.append(jnp.concatenate(grads_list, axis=-1))
            per_expert = jnp.stack(partial_list)
            token_part = jnp.einsum("scte,esc->ste", select, per_expert, precision=highest).reshape(TOKENS, EXPERTS)
            pair_part = jnp.sum(onehot * token_part[:, None, :], axis=-1)
            mixed = jnp.sum(gate_prob * pair_part, axis=-1, keepdims=True)
            logit_grad = gate_prob * (pair_part - mixed)
            spread = jnp.sum(onehot * logit_grad[:, :, None], axis=1)
            router_term = jnp.dot(spread, router_weight[section_id].T, precision=highest)
            micro_inputs.append((out_grad.astype(jnp.float32) + router_term).astype(jnp.bfloat16))
        section_grads.append(jnp.stack(micro_grads))
        section_inputs.append(jnp.stack(micro_inputs))
    hidden_grad = jnp.stack(section_grads)
    inputs_all = jnp.stack(section_inputs)
    upstream_grad = jnp.concatenate([inputs_all[1:], jnp.zeros_like(inputs_all[:1])], axis=0)
    return (hidden_grad, upstream_grad)
```

```python
import functools

import jax
import jax.numpy as jnp
from jax import lax
from jax.experimental import pallas as pl
from jax.experimental.pallas import tpu as pltpu
from jax.sharding import PartitionSpec as P

VMEM = pltpu.VMEM
HIGHEST = lax.Precision.HIGHEST
MIB = 1024 * 1024
SCALE = 0.001


def whole():
    return pl.BlockSpec(memory_space=VMEM)


def in_hbm():
    return pl.BlockSpec(memory_space=pltpu.HBM)


def cost(flops):
    return pl.CostEstimate(flops=max(1, int(SCALE * flops)), bytes_accessed=1, transcendentals=0)


def scalars():
    return pl.BlockSpec(memory_space=pltpu.SMEM)


def routing(small, expert0, experts, tok, cap, micro):
    total = small.shape[1]
    id0, id1 = small[0:1], small[1:2]
    gate0 = jax.nn.sigmoid(small[2:3] - small[3:4])
    gate1 = jax.nn.sigmoid(small[3:4] - small[2:3])
    names = []
    for k in range(experts):
        e = lax.rem(expert0 + k, experts).astype(jnp.float32)
        names.append(((id0 == e).astype(jnp.float32), (id1 == e).astype(jnp.float32)))
    hits = jnp.concatenate([a + b for a, b in names] * (8 // experts), axis=0)
    before = lax.broadcasted_iota(jnp.int32, (total, total), 0)
    after = lax.broadcasted_iota(jnp.int32, (total, total), 1)
    same = (before < after) & (before // tok == after // tok)
    ranks = jnp.dot(
        hits.astype(jnp.bfloat16),
        same.astype(jnp.float32).astype(jnp.bfloat16),
        preferred_element_type=jnp.float32,
    )
    row = lax.broadcasted_iota(jnp.int32, (micro * cap, total), 0)
    token = lax.broadcasted_iota(jnp.int32, (micro * cap, total), 1)
    slot = (row % cap).astype(jnp.float32)
    same_micro = row // cap == token // tok
    picks = []
    for k in range(experts):
        mask = (ranks[k : k + 1] == slot) & (hits[k : k + 1] > 0) & same_micro
        picks.append(mask.astype(jnp.float32))
    return picks, names, (gate0, gate1)


def first_pack_kernel(dims, g_ref, ids_ref, logits_ref, dy_ref, *outs):
    experts, tok, cap, micro = dims
    lines = []
    for ref in (ids_ref, logits_ref):
        for side in range(2):
            parts = [ref[m, side : side + 1, :].astype(jnp.float32) for m in range(micro)]
            lines.append(jnp.concatenate(parts, axis=1))
    small = jnp.concatenate(lines + lines, axis=0)
    picks, names, gates = routing(small, g_ref[0], experts, tok, cap, micro)
    rows = micro * cap
    flat = jnp.concatenate(picks, axis=0).astype(jnp.bfloat16)
    block = jnp.dot(flat, dy_ref[...], preferred_element_type=jnp.float32)
    width = dy_ref.shape[1]
    for k in range(experts):
        outs[k][:, 0:width] = block[k * rows : (k + 1) * rows].astype(jnp.bfloat16)
        gate = names[k][0] * gates[0] + names[k][1] * gates[1]
        slot_gate = jnp.sum(picks[k] * gate, axis=1, keepdims=True)
        outs[k][:, width:] = jnp.broadcast_to(slot_gate, (rows, 128)).astype(jnp.bfloat16)
    outs[-2][...] = small
    outs[-1][...] = flat


def first_pack(dims, width, g, ids, logits, dy):
    experts, tok, cap, micro = dims
    rows = micro * cap
    tokens = dy.shape[0]
    shapes = [jax.ShapeDtypeStruct((rows, width + 128), jnp.bfloat16)] * experts
    shapes += [
        jax.ShapeDtypeStruct((8, tokens), jnp.float32),
        jax.ShapeDtypeStruct((experts * rows, tokens), jnp.bfloat16),
    ]
    return pl.pallas_call(
        functools.partial(first_pack_kernel, dims),
        grid=(1,),
        in_specs=[scalars(), whole(), whole(), pl.BlockSpec((tokens, width), lambda i: (0, 0))],
        out_specs=[whole()] * len(shapes),
        out_shape=shapes,
        compiler_params=pltpu.CompilerParams(vmem_limit_bytes=16 * MIB),
        cost_estimate=cost(1),
        name="pack_first",
    )(g, ids, logits, dy)


def rest_pack_kernel(experts, rows, offsets, widths, flat_ref, dy_ref, *outs):
    flat = flat_ref[...]
    for n, (offset, width) in enumerate(zip(offsets, widths)):
        block = jnp.dot(flat, dy_ref[:, offset : offset + width], preferred_element_type=jnp.float32)
        for k in range(experts):
            outs[n * experts + k][...] = block[k * rows : (k + 1) * rows].astype(jnp.bfloat16)


def rest_pack(experts, rows, offsets, widths, flat, dy):
    shapes = [
        jax.ShapeDtypeStruct((rows, width), jnp.bfloat16) for width in widths for _ in range(experts)
    ]
    return pl.pallas_call(
        functools.partial(rest_pack_kernel, experts, rows, offsets, widths),
        in_specs=[whole(), whole()],
        out_specs=[whole()] * len(shapes),
        out_shape=shapes,
        compiler_params=pltpu.CompilerParams(vmem_limit_bytes=24 * MIB),
        cost_estimate=cost(1),
        name="pack_rest",
    )(flat, dy)


def saved_kernel(experts, groups, lane, offset, cuts, pos_ref, saved_ref, w_ref, *refs):
    ys, perm_ref, back_ref = refs[:groups], refs[groups], refs[groups + 1]
    saved_buf, w_buf, saved_sem, w_sem = refs[groups + 2 :]
    spans = list(zip(cuts[:-1], cuts[1:]))
    width = w_buf.shape[1]

    def fetch_saved(i):
        low, high = spans[i]
        return pltpu.make_async_copy(saved_ref.at[:, low:high], saved_buf.at[:, low:high], saved_sem.at[i])

    def fetch_weight(i):
        low, high = spans[i]
        return pltpu.make_async_copy(
            w_ref.at[low:high, offset : offset + width], w_buf.at[low:high, :], w_sem.at[i]
        )

    for i in range(len(spans)):
        fetch_saved(i).start()
        fetch_weight(i).start()

    rows = perm_ref.shape[0]
    sources = experts * groups
    each = rows // sources
    g, c = pos_ref[0], pos_ref[1]

    def target(dim, shape):
        at = lax.broadcasted_iota(jnp.int32, shape, dim)
        block = at // each
        source = jnp.zeros(shape, jnp.int32)
        for q in range(groups):
            for k in range(experts):
                j = lax.rem(g + experts - k, experts) * groups + lax.rem(c + groups - q, groups)
                source = jnp.where(block == q * experts + k, j, source)
        return (at - block * each) * sources + source

    span = 48 if rows % 48 == 0 else 16
    lanes = target(1, (1, rows))
    plain = lax.broadcasted_iota(jnp.int32, (span, rows), 1)
    for s in range(rows // span):
        at = lax.broadcasted_iota(jnp.int32, (span, rows), 0) + s * span
        perm_ref[s * span : (s + 1) * span, :] = (at == lanes).astype(jnp.float32).astype(jnp.bfloat16)
    column = target(0, (rows, 128))
    for s in range(rows // span):
        there = column[s * span : (s + 1) * span, 0:1]
        back_ref[s * span : (s + 1) * span, :] = (plain == there).astype(jnp.float32).astype(jnp.bfloat16)

    total = None
    for i, (low, high) in enumerate(spans):
        fetch_saved(i).wait()
        fetch_weight(i).wait()
        part = jnp.dot(saved_buf[:, low:high], w_buf[low:high, :], preferred_element_type=jnp.float32)
        total = part if total is None else total + part
    ordered = exact_rows(back_ref[...], total, 2)
    for q in range(groups):
        ys[q][...] = ordered[q * lane : (q + 1) * lane]


def exact_rows(matrix, value, parts):
    total = None
    for _ in range(parts):
        piece = value.astype(jnp.bfloat16)
        value = value - piece.astype(jnp.float32)
        term = jnp.dot(matrix, piece, preferred_element_type=jnp.float32)
        total = term if total is None else total + term
    return total


def saved_forward(experts, groups, pos, saved, weight, offset, width, cuts):
    rows, hidden = saved.shape
    lane = rows // groups
    shapes = [jax.ShapeDtypeStruct((lane, width), jnp.float32)] * groups
    shapes += [jax.ShapeDtypeStruct((rows, rows), jnp.bfloat16)] * 2
    return pl.pallas_call(
        functools.partial(saved_kernel, experts, groups, lane, offset, cuts),
        in_specs=[scalars(), in_hbm(), in_hbm()],
        out_specs=[whole()] * len(shapes),
        out_shape=shapes,
        scratch_shapes=[
            VMEM((rows, hidden), jnp.bfloat16),
            VMEM((hidden, width), jnp.bfloat16),
            pltpu.SemaphoreType.DMA((len(cuts) - 1,)),
            pltpu.SemaphoreType.DMA((len(cuts) - 1,)),
        ],
        compiler_params=pltpu.CompilerParams(vmem_limit_bytes=62 * MIB - 4 * lane * groups * width - 4 * rows * rows),
        cost_estimate=cost(2 * rows * hidden * width),
        name="saved_times_weight",
    )(pos, saved, weight)


def chunk_kernel(stage, pieces, lane, offset, width, cuts, *refs):
    refs = list(refs)
    x_refs = [refs.pop(0) for _ in range(pieces)]
    perm_ref, w_ref = refs.pop(0), refs.pop(0)
    if stage == "last":
        acc_in, gate_ref, out_ref, _, x_all, w_buf, w_sem, out_buf, out_sem = refs
    elif stage == "dots":
        acc_in, saved_ref, back_ref, acc_ref = refs[:4]
        early_refs, (x_all, w_buf, w_sem, saved_buf, saved_sem) = refs[4:-5], refs[-5:]
    elif stage == "middle":
        acc_in, acc_ref, x_all, w_buf, w_sem = refs
    else:
        acc_ref, gate_ref, x_all, w_buf, w_sem = refs
    spans = list(zip(cuts[:-1], cuts[1:]))

    def fetch(i):
        low, high = spans[i]
        return pltpu.make_async_copy(
            w_ref.at[low:high, offset : offset + width], w_buf.at[low:high, :], w_sem.at[i]
        )

    def send(i):
        low, high = spans[i]
        return pltpu.make_async_copy(out_buf.at[:, low:high], out_ref.at[:, low:high], out_sem.at[i])

    def fetch_saved(i):
        low, high = spans[i]
        return pltpu.make_async_copy(saved_ref.at[:, low:high], saved_buf.at[:, low:high], saved_sem.at[i])

    for i in range(len(spans)):
        fetch(i).start()
        if stage == "dots":
            fetch_saved(i).start()
    mixed = jnp.concatenate([r[...].astype(jnp.float32) for r in x_refs], axis=0).astype(jnp.bfloat16)
    mixed = jnp.dot(perm_ref[...], mixed, preferred_element_type=jnp.float32)
    x_all[...] = mixed[:, 0:width].astype(jnp.bfloat16)
    if stage == "first":
        gate_ref[...] = mixed[:, width:]
    if stage == "last":
        gate = gate_ref[:, 0:1]
    dots = None
    for i, (low, high) in enumerate(spans):
        fetch(i).wait()
        raw = lax.dot_general(
            x_all[...], w_buf[low:high, :], (((1,), (1,)), ((), ())), preferred_element_type=jnp.float32
        )
        if stage != "first":
            raw = acc_in[:, low:high] + raw
        if stage == "last":
            out_buf[:, low:high] = (raw * gate).astype(jnp.bfloat16)
            send(i).start()
        else:
            acc_ref[:, low:high] = raw
        if stage == "dots":
            fetch_saved(i).wait()
            product = raw * saved_buf[:, low:high].astype(jnp.float32)
            for at in range(0, high - low, 128):
                piece = product[:, at : at + 128]
                dots = piece if dots is None else dots + piece
    if stage == "dots":
        total = jnp.sum(dots, axis=1, keepdims=True)
        ordered = exact_rows(back_ref[...], jnp.broadcast_to(total, dots.shape), 3)
        for q, ref in enumerate(early_refs):
            ref[...] = ordered[q * lane : (q + 1) * lane]
    if stage == "last":
        for i in range(len(spans)):
            send(i).wait()


def cut(total, parts):
    points = [0]
    for part in parts:
        points.append(points[-1] + total * part // sum(parts))
    return points


def room(stage, rows, hidden, width, cuts):
    span = max(b - a for a, b in zip(cuts[:-1], cuts[1:]))
    each = 8 if rows <= 1024 else 14
    total = hidden * width * 2 + rows * width * each + rows * span * 8 + 3 * MIB
    if stage in ("dots", "last"):
        total += rows * hidden * 2
    if stage == "dots":
        total += rows * 128 * 24
    return total


def chunk(stage, groups, offset, width, cuts, weight, xs, perm, acc=None, saved=None, back=None, gate=None):
    hidden = weight.shape[0]
    rows = sum(x.shape[0] for x in xs)
    lane = rows // groups
    operands = list(xs) + [perm, weight]
    specs = [whole()] * (len(xs) + 1) + [in_hbm()]
    aliases = {}
    acc_shape = jax.ShapeDtypeStruct((rows, hidden), jnp.float32)
    if stage != "first":
        aliases = {len(operands): 1 if stage == "last" else 0}
        operands.append(acc)
        specs.append(whole())
    scratch = [
        VMEM((rows, width), jnp.bfloat16),
        VMEM((hidden, width), jnp.bfloat16),
        pltpu.SemaphoreType.DMA((len(cuts) - 1,)),
    ]
    if stage == "dots":
        operands += [saved, back]
        specs += [in_hbm(), whole()]
        scratch += [VMEM((rows, hidden), jnp.bfloat16), pltpu.SemaphoreType.DMA((len(cuts) - 1,))]
        out_shape = [acc_shape] + [jax.ShapeDtypeStruct((lane, 128), jnp.float32)] * groups
        out_specs = [whole()] * len(out_shape)
    elif stage == "last":
        operands.append(gate)
        specs.append(whole())
        out_shape = [jax.ShapeDtypeStruct((rows, hidden), jnp.bfloat16), acc_shape]
        out_specs = [in_hbm(), whole()]
        scratch += [VMEM((rows, hidden), jnp.bfloat16), pltpu.SemaphoreType.DMA((len(cuts) - 1,))]
    elif stage == "first":
        out_shape = [acc_shape, jax.ShapeDtypeStruct((rows, 128), jnp.float32)]
        out_specs = [whole(), whole()]
    else:
        out_shape, out_specs = acc_shape, whole()
    return pl.pallas_call(
        functools.partial(chunk_kernel, stage, len(xs), lane, offset, width, cuts),
        in_specs=specs,
        out_specs=out_specs,
        out_shape=out_shape,
        scratch_shapes=scratch,
        input_output_aliases=aliases,
        compiler_params=pltpu.CompilerParams(vmem_limit_bytes=room(stage, rows, hidden, width, cuts)),
        cost_estimate=cost(2 * rows * hidden * width),
        name="chunk_" + stage,
    )(*operands)


def dots_kernel(experts, rows, groups, *refs):
    x_refs = refs[:experts]
    y_refs = refs[experts : experts + groups]
    early_refs = refs[experts + groups : experts + 2 * groups]
    outs = refs[experts + 2 * groups :]
    for k in range(experts):
        span = slice(k * rows, (k + 1) * rows)
        y = y_refs[0][span, :]
        early = early_refs[0][span, :]
        for other in range(1, groups):
            y = y + y_refs[other][span, :]
            early = early + early_refs[other][span, :]
        late = jnp.sum(x_refs[k][...].astype(jnp.float32) * y, axis=1, keepdims=True)
        outs[k][...] = jnp.transpose(early + late)[0:8]


def late_dots(experts, groups, xs, ys, earlies):
    rows = xs[0].shape[0]
    lane = experts * rows
    return pl.pallas_call(
        functools.partial(dots_kernel, experts, rows, groups),
        in_specs=[whole()] * (experts + 2 * groups),
        out_specs=[whole()] * experts,
        out_shape=[jax.ShapeDtypeStruct((8, rows), jnp.float32)] * experts,
        compiler_params=pltpu.CompilerParams(vmem_limit_bytes=16 * MIB),
        cost_estimate=cost(1),
        name="gate_dots",
    )(*xs, *ys, *earlies)


def plan_kernel(dims, g_ref, extra_ref, pick_ref, token_ref):
    experts, tok, cap, micro = dims
    total = micro * tok
    small = extra_ref[experts : experts + 4, 0:total]
    picks, names, gates = routing(small, g_ref[0], experts, tok, cap, micro)
    for k in range(experts):
        both = jnp.concatenate([picks[k] * names[k][0], picks[k] * names[k][1]], axis=1)
        pick_ref[k] = both.astype(jnp.bfloat16)
    lines = list(gates)
    for side in range(2):
        for e in range(experts):
            lines.append((small[side : side + 1] == e).astype(jnp.float32))
    lines.append(jnp.zeros((128 - len(lines), total), jnp.float32))
    token_ref[...] = jnp.transpose(jnp.concatenate(lines, axis=0))


def plan(dims, g, extra):
    experts, tok, cap, micro = dims
    total = micro * tok
    return pl.pallas_call(
        functools.partial(plan_kernel, dims),
        in_specs=[scalars(), whole()],
        out_specs=[whole(), whole()],
        out_shape=[
            jax.ShapeDtypeStruct((experts, micro * cap, 2 * total), jnp.bfloat16),
            jax.ShapeDtypeStruct((total, 128), jnp.float32),
        ],
        compiler_params=pltpu.CompilerParams(vmem_limit_bytes=16 * MIB),
        cost_estimate=cost(1),
        name="plan",
    )(g, extra)


def final_kernel(experts, pick_ref, token_ref, router_ref, dy_ref, *refs):
    dot_refs, out_ref = refs[:experts], refs[experts]
    total = dy_ref.shape[0]
    pair = None
    for k in range(experts):
        line = dot_refs[k][0:1]
        parts = []
        for _ in range(3):
            piece = line.astype(jnp.bfloat16).astype(jnp.float32)
            line = line - piece
            parts.append(piece)
        parts.append(jnp.zeros((5, line.shape[1]), jnp.float32))
        rows = jnp.concatenate(parts, axis=0).astype(jnp.bfloat16)
        term = lax.dot_general(
            pick_ref[k], rows, (((0,), (1,)), ((), ())), preferred_element_type=jnp.float32
        )
        pair = term if pair is None else pair + term
    pair = pair[:, 0:1] + pair[:, 1:2] + pair[:, 2:3]
    pair0, pair1 = pair[0:total], pair[total : 2 * total]
    gate0, gate1 = token_ref[:, 0:1], token_ref[:, 1:2]
    mixed = gate0 * pair0 + gate1 * pair1
    grad0 = gate0 * (pair0 - mixed)
    grad1 = gate1 * (pair1 - mixed)
    spread = []
    for e in range(experts):
        spread.append(
            token_ref[:, 2 + e : 3 + e] * grad0 + token_ref[:, 2 + experts + e : 3 + experts + e] * grad1
        )
    width = 512
    for at in range(0, dy_ref.shape[1], width):
        value = dy_ref[:, at : at + width].astype(jnp.float32)
        term = spread[0] * router_ref[0:1, at : at + width]
        for e in range(1, experts):
            term = term + spread[e] * router_ref[e : e + 1, at : at + width]
        out_ref[:, at : at + width] = (value + term).astype(jnp.bfloat16)


def finish(experts, pick, token, router, dy, dots):
    return pl.pallas_call(
        functools.partial(final_kernel, experts),
        in_specs=[whole()] * (4 + experts),
        out_specs=whole(),
        out_shape=jax.ShapeDtypeStruct(dy.shape, jnp.bfloat16),
        compiler_params=pltpu.CompilerParams(vmem_limit_bytes=16 * MIB),
        cost_estimate=cost(1),
        name="input_grad",
    )(pick, token, router, dy, *dots)


def after(value, *others):
    return lax.optimization_barrier((value,) + others)[0]


def local(upstream_dy, gate_logits, expert_ids, saved_hidden, down_weight, router_weight):
    devices = lax.axis_size("expert")
    sections = lax.axis_size("section")
    _, micro, tok, width = upstream_dy.shape
    experts = router_weight.shape[2]
    cap = saved_hidden.shape[3]
    groups = devices // experts
    hidden = down_weight.shape[1]
    rows = micro * cap
    dims = (experts, tok, cap, micro)
    index = lax.axis_index("expert")
    g, c = index // groups, index % groups
    g_op = jnp.reshape(g, (1,)).astype(jnp.int32)
    pos = jnp.stack([g, c]).astype(jnp.int32)

    def to_chip(value, k):
        return lax.ppermute(
            value, "expert", [(i, (i + k * groups) % devices) for i in range(devices)]
        )

    def to_member(value, r):
        return lax.ppermute(
            value,
            "expert",
            [(i, i // groups * groups + (i % groups + r) % groups) for i in range(devices)],
        )

    def to_previous(value):
        return lax.ppermute(value, "section", [(s, s - 1) for s in range(1, sections)])

    def dots_home(value, k):
        pairs = []
        for s in range(1, sections):
            for i in range(devices):
                pairs.append((s * devices + i, (s - 1) * devices + (i + devices - k * groups) % devices))
        return lax.ppermute(value, ("section", "expert"), pairs)

    tokens = micro * tok
    dy = upstream_dy.reshape(tokens, width)
    weight = down_weight[0]
    saved = saved_hidden[0].transpose(0, 2, 1, 3).reshape(-1, hidden)

    part = width // 12
    widths = [3 * part, 4 * part, 3 * part, 2 * part] if devices * rows <= 1024 else [part] * 12
    offsets = [sum(widths[:n]) for n in range(len(widths))]
    count = len(widths)
    first = first_pack(
        dims,
        widths[0],
        g_op,
        expert_ids[0].transpose(0, 2, 1),
        gate_logits[0].transpose(0, 2, 1),
        dy,
    )
    small, slot_matrix = first[-2], first[-1]
    rest = rest_pack(experts, rows, offsets[1:], widths[1:], slot_matrix, dy)
    sends = [first[:experts]] + [rest[n * experts : (n + 1) * experts] for n in range(count - 1)]

    order = [2, 1, 3] if experts == 4 else list(range(1, experts))

    def travel(n, *others):
        here = [sends[n][0]] + [None] * (experts - 1)
        for k in order:
            value = sends[n][k]
            if n > 0:
                value = after(value, *others)
            here[k] = to_chip(value, k)
        got.append(here)

    def both(here, *others):
        out = [after(piece, *others) for piece in here]
        return here + [to_member(piece, r) for r in range(1, groups) for piece in out]

    got = []
    travel(0)
    travel(1)
    extra = jnp.pad(small[0:4], ((0, 0), (0, width - tokens)))
    extra_next = to_previous(jnp.concatenate([router_weight[0].T, extra], axis=0))
    dy_next = to_previous(after(dy, slot_matrix))

    cuts = cut(hidden, (1, 1, 2, 2, 2))
    made = saved_forward(experts, groups, after(pos, rest[0]), saved, weight, offsets[-1], widths[-1], cuts)
    ys, perm, back = made[:groups], made[groups], made[groups + 1]
    ys = [ys[0]] + [to_member(ys[q], -q) for q in range(1, groups)]
    pick, token = plan(dims, g_op, extra_next)

    acc = perm
    for n in range(count - 1):
        xs = both(got[n], acc, pick)
        if n == 0:
            acc, gate = chunk("first", groups, offsets[n], widths[n], cuts, weight, xs, perm)
        elif n < count - 2:
            acc = chunk("middle", groups, offsets[n], widths[n], cuts, weight, xs, perm, acc=acc)
        else:
            acc, *early = chunk(
                "dots", groups, offsets[n], widths[n], cuts, weight, xs, perm, acc=acc, saved=saved, back=back
            )
        if n + 2 < count:
            travel(n + 2, acc)
    earlies = [early[0]] + [to_member(early[q], -q) for q in range(1, groups)]
    xs = both(got[-1], acc)
    dots = late_dots(experts, groups, got[-1], ys, earlies)
    homes = [dots_home(dots[k], k) for k in range(experts)]
    hidden_grad, _ = chunk(
        "last", groups, offsets[-1], widths[-1], cuts, weight, xs, perm, acc=acc, gate=gate
    )
    result = finish(experts, pick, token, extra_next, dy_next, homes)
    hidden_grad = hidden_grad.reshape(micro, cap, devices, hidden).transpose(0, 2, 1, 3)
    return (hidden_grad[None], result.reshape(upstream_dy.shape))


def solution(mesh):
    placed = (
        P("section", None, "expert", None),
        P("section", None, "expert", None),
        P("section", None, "expert", None),
        P("section", None, None, None, "expert"),
        P("section", "expert", None),
        P("section", None, None),
    )
    return jax.shard_map(
        local,
        mesh=mesh,
        in_specs=placed,
        out_specs=(P("section", None, None, None, "expert"), P("section", None, "expert", None)),
        check_vma=False,
    )
```

```python
import functools

import jax
import jax.numpy as jnp
from jax import lax
from jax.experimental import pallas as pl
from jax.experimental.pallas import tpu as pltpu
from jax.sharding import PartitionSpec as P

VMEM = pltpu.VMEM
HIGHEST = lax.Precision.HIGHEST
MIB = 1024 * 1024
SCALE = 0.001


def whole():
    return pl.BlockSpec(memory_space=VMEM)


def in_hbm():
    return pl.BlockSpec(memory_space=pltpu.HBM)


def cost(flops):
    return pl.CostEstimate(flops=max(1, int(SCALE * flops)), bytes_accessed=1, transcendentals=0)


def routing(small, expert0, experts, tok, cap, micro):
    total = small.shape[1]
    id0, id1 = small[0:1], small[1:2]
    gate0 = jax.nn.sigmoid(small[2:3] - small[3:4])
    gate1 = jax.nn.sigmoid(small[3:4] - small[2:3])
    names = []
    for k in range(experts):
        e = lax.rem(expert0 + k, experts).astype(jnp.float32)
        names.append(((id0 == e).astype(jnp.float32), (id1 == e).astype(jnp.float32)))
    hits = jnp.concatenate([a + b for a, b in names] * (8 // experts), axis=0)
    before = lax.broadcasted_iota(jnp.int32, (total, total), 0)
    after = lax.broadcasted_iota(jnp.int32, (total, total), 1)
    same = (before < after) & (before // tok == after // tok)
    ranks = jnp.dot(
        hits.astype(jnp.bfloat16),
        same.astype(jnp.float32).astype(jnp.bfloat16),
        preferred_element_type=jnp.float32,
    )
    row = lax.broadcasted_iota(jnp.int32, (micro * cap, total), 0)
    token = lax.broadcasted_iota(jnp.int32, (micro * cap, total), 1)
    slot = (row % cap).astype(jnp.float32)
    same_micro = row // cap == token // tok
    picks = []
    for k in range(experts):
        mask = (ranks[k : k + 1] == slot) & (hits[k : k + 1] > 0) & same_micro
        picks.append(mask.astype(jnp.float32))
    return picks, names, (gate0, gate1)


def first_pack_kernel(dims, groups, ids_ref, logits_ref, dy_ref, *outs):
    experts, tok, cap, micro = dims
    lines = []
    for ref in (ids_ref, logits_ref):
        for side in range(2):
            parts = [ref[m, side : side + 1, :].astype(jnp.float32) for m in range(micro)]
            lines.append(jnp.concatenate(parts, axis=1))
    small = jnp.concatenate(lines + lines, axis=0)
    picks, names, gates = routing(small, place(experts, groups)[0], experts, tok, cap, micro)
    rows = micro * cap
    flat = jnp.concatenate(picks, axis=0).astype(jnp.bfloat16)
    block = jnp.dot(flat, dy_ref[...], preferred_element_type=jnp.float32)
    width = dy_ref.shape[1]
    for k in range(experts):
        outs[k][:, 0:width] = block[k * rows : (k + 1) * rows].astype(jnp.bfloat16)
        gate = names[k][0] * gates[0] + names[k][1] * gates[1]
        slot_gate = jnp.sum(picks[k] * gate, axis=1, keepdims=True)
        outs[k][:, width:] = jnp.broadcast_to(slot_gate, (rows, 128)).astype(jnp.bfloat16)
    outs[-2][...] = small
    outs[-1][...] = flat


def first_pack(dims, groups, width, ids, logits, dy):
    experts, tok, cap, micro = dims
    rows = micro * cap
    tokens = dy.shape[0]
    shapes = [jax.ShapeDtypeStruct((rows, width + 128), jnp.bfloat16)] * experts
    shapes += [
        jax.ShapeDtypeStruct((8, tokens), jnp.float32),
        jax.ShapeDtypeStruct((experts * rows, tokens), jnp.bfloat16),
    ]
    return pl.pallas_call(
        functools.partial(first_pack_kernel, dims, groups),
        grid=(1,),
        in_specs=[whole(), whole(), pl.BlockSpec((tokens, width), lambda i: (0, 0))],
        out_specs=[whole()] * len(shapes),
        out_shape=shapes,
        compiler_params=pltpu.CompilerParams(vmem_limit_bytes=16 * MIB),
        cost_estimate=cost(1),
        name="pack_first",
    )(ids, logits, dy)


def rest_pack_kernel(experts, rows, offsets, widths, flat_ref, dy_ref, small_ref, router_ref, *outs):
    flat = flat_ref[...]
    outs[-1][0:experts, :] = router_ref[...]
    outs[-1][experts:, :] = jnp.zeros((outs[-1].shape[0] - experts, dy_ref.shape[1]), jnp.float32)
    outs[-1][experts : experts + 4, 0 : small_ref.shape[1]] = small_ref[0:4]
    for n, (offset, width) in enumerate(zip(offsets, widths)):
        block = jnp.dot(flat, dy_ref[:, offset : offset + width], preferred_element_type=jnp.float32)
        for k in range(experts):
            outs[n * experts + k][...] = block[k * rows : (k + 1) * rows].astype(jnp.bfloat16)


def rest_pack(experts, rows, offsets, widths, flat, dy, small, router):
    shapes = [
        jax.ShapeDtypeStruct((rows, width), jnp.bfloat16) for width in widths for _ in range(experts)
    ]
    shapes.append(jax.ShapeDtypeStruct((experts + 4, dy.shape[1]), jnp.float32))
    return pl.pallas_call(
        functools.partial(rest_pack_kernel, experts, rows, offsets, widths),
        in_specs=[whole()] * 4,
        out_specs=[whole()] * len(shapes),
        out_shape=shapes,
        compiler_params=pltpu.CompilerParams(vmem_limit_bytes=24 * MIB),
        cost_estimate=cost(1),
        name="pack_rest",
    )(flat, dy, small, router)


def saved_kernel(experts, groups, lane, offset, cuts, _, saved_ref, w_ref, *refs):
    ys, perm_ref, back_ref = refs[:groups], refs[groups], refs[groups + 1]
    saved_buf, w_buf, saved_sem, w_sem = refs[groups + 2 :]
    spans = list(zip(cuts[:-1], cuts[1:]))
    width = w_buf.shape[1]

    def fetch_saved(i):
        low, high = spans[i]
        return pltpu.make_async_copy(saved_ref.at[:, low:high], saved_buf.at[:, low:high], saved_sem.at[i])

    def fetch_weight(i):
        low, high = spans[i]
        return pltpu.make_async_copy(
            w_ref.at[low:high, offset : offset + width], w_buf.at[low:high, :], w_sem.at[i]
        )

    for i in range(len(spans)):
        fetch_saved(i).start()
        fetch_weight(i).start()

    rows = perm_ref.shape[0]
    sources = experts * groups
    each = rows // sources
    g, c = place(experts, groups)

    def target(dim, shape):
        at = lax.broadcasted_iota(jnp.int32, shape, dim)
        block = at // each
        source = jnp.zeros(shape, jnp.int32)
        for q in range(groups):
            for k in range(experts):
                j = lax.rem(g + experts - k, experts) * groups + lax.rem(c + groups - q, groups)
                source = jnp.where(block == q * experts + k, j, source)
        return (at - block * each) * sources + source

    span = 48 if rows % 48 == 0 else 16
    lanes = target(1, (1, rows))
    plain = lax.broadcasted_iota(jnp.int32, (span, rows), 1)
    for s in range(rows // span):
        at = lax.broadcasted_iota(jnp.int32, (span, rows), 0) + s * span
        perm_ref[s * span : (s + 1) * span, :] = (at == lanes).astype(jnp.float32).astype(jnp.bfloat16)
    column = target(0, (rows, 128))
    for s in range(rows // span):
        there = column[s * span : (s + 1) * span, 0:1]
        back_ref[s * span : (s + 1) * span, :] = (plain == there).astype(jnp.float32).astype(jnp.bfloat16)

    total = None
    for i, (low, high) in enumerate(spans):
        fetch_saved(i).wait()
        fetch_weight(i).wait()
        part = jnp.dot(saved_buf[:, low:high], w_buf[low:high, :], preferred_element_type=jnp.float32)
        total = part if total is None else total + part
    ordered = exact_rows(back_ref[...], total, 2)
    for q in range(groups):
        ys[q][...] = ordered[q * lane : (q + 1) * lane]


def place(experts, groups):
    index = lax.axis_index("expert")
    return index // groups, index % groups


def exact_rows(matrix, value, parts):
    total = None
    for _ in range(parts):
        piece = value.astype(jnp.bfloat16)
        value = value - piece.astype(jnp.float32)
        term = jnp.dot(matrix, piece, preferred_element_type=jnp.float32)
        total = term if total is None else total + term
    return total


def saved_forward(experts, groups, first, saved, weight, offset, width, cuts):
    rows, hidden = saved.shape
    lane = rows // groups
    shapes = [jax.ShapeDtypeStruct((lane, width), jnp.float32)] * groups
    shapes += [jax.ShapeDtypeStruct((rows, rows), jnp.bfloat16)] * 2
    return pl.pallas_call(
        functools.partial(saved_kernel, experts, groups, lane, offset, cuts),
        in_specs=[in_hbm()] * 3,
        out_specs=[whole()] * len(shapes),
        out_shape=shapes,
        scratch_shapes=[
            VMEM((rows, hidden), jnp.bfloat16),
            VMEM((hidden, width), jnp.bfloat16),
            pltpu.SemaphoreType.DMA((len(cuts) - 1,)),
            pltpu.SemaphoreType.DMA((len(cuts) - 1,)),
        ],
        compiler_params=pltpu.CompilerParams(vmem_limit_bytes=(119 if rows <= 1024 else 125) * (MIB // 2) - 4 * lane * groups * width - 4 * rows * rows),
        cost_estimate=cost(2 * rows * hidden * width),
        name="saved_times_weight",
    )(first, saved, weight)


def chunk_kernel(stage, pieces, lane, offset, width, cuts, *refs):
    refs = list(refs)
    x_refs = [refs.pop(0) for _ in range(pieces)]
    perm_ref, w_ref = refs.pop(0), refs.pop(0)
    if stage == "last":
        acc_in, gate_ref, out_ref, _, x_all, w_buf, w_sem, out_buf, out_sem = refs
    elif stage == "dots":
        acc_in, saved_ref, back_ref, acc_ref = refs[:4]
        early_refs, (x_all, w_buf, w_sem, saved_buf, saved_sem) = refs[4:-5], refs[-5:]
    elif stage == "middle":
        acc_in, acc_ref, x_all, w_buf, w_sem = refs
    else:
        acc_ref, gate_ref, x_all, w_buf, w_sem = refs
    spans = list(zip(cuts[:-1], cuts[1:]))

    def fetch(i):
        low, high = spans[i]
        return pltpu.make_async_copy(
            w_ref.at[low:high, offset : offset + width], w_buf.at[low:high, :], w_sem.at[i]
        )

    def send(i):
        low, high = spans[i]
        return pltpu.make_async_copy(out_buf.at[:, low:high], out_ref.at[:, low:high], out_sem.at[i])

    def fetch_saved(i):
        low, high = spans[i]
        return pltpu.make_async_copy(saved_ref.at[:, low:high], saved_buf.at[:, low:high], saved_sem.at[i])

    for i in range(len(spans)):
        fetch(i).start()
        if stage == "dots":
            fetch_saved(i).start()
    values = [r[...].astype(jnp.float32) for r in x_refs]
    mixed = jnp.concatenate(values, axis=0).astype(jnp.bfloat16)
    mixed = jnp.dot(perm_ref[...], mixed, preferred_element_type=jnp.float32)
    x_all[...] = mixed[:, 0:width].astype(jnp.bfloat16)
    if stage == "first":
        gate_ref[...] = mixed[:, width:]
    if stage == "last":
        gate = gate_ref[:, 0:1]
    dots = None
    for i, (low, high) in enumerate(spans):
        fetch(i).wait()
        raw = lax.dot_general(
            x_all[...], w_buf[low:high, :], (((1,), (1,)), ((), ())), preferred_element_type=jnp.float32
        )
        if stage != "first":
            raw = acc_in[:, low:high] + raw
        if stage == "last":
            out_buf[:, low:high] = (raw * gate).astype(jnp.bfloat16)
            send(i).start()
        else:
            acc_ref[:, low:high] = raw
        if stage == "dots":
            fetch_saved(i).wait()
            product = raw * saved_buf[:, low:high].astype(jnp.float32)
            for at in range(0, high - low, 128):
                piece = product[:, at : at + 128]
                dots = piece if dots is None else dots + piece
    if stage == "dots":
        total = jnp.sum(dots, axis=1, keepdims=True)
        ordered = exact_rows(back_ref[...], jnp.broadcast_to(total, dots.shape), 3)
        for q, ref in enumerate(early_refs):
            ref[...] = ordered[q * lane : (q + 1) * lane]
    if stage == "last":
        for i in range(len(spans)):
            send(i).wait()


def cut(total, parts):
    points = [0]
    for part in parts:
        points.append(points[-1] + total * part // sum(parts))
    return points


def room(stage, rows, hidden, width, cuts):
    span = max(b - a for a, b in zip(cuts[:-1], cuts[1:]))
    each = 8 if rows <= 1024 else 14
    total = hidden * width * 2 + rows * width * each + rows * span * 8 + 3 * MIB
    if stage in ("dots", "last"):
        total += rows * hidden * 2
    if stage == "dots":
        total += rows * 128 * 24
    return total


def chunk(stage, groups, offset, width, cuts, weight, xs, perm, acc=None, saved=None, back=None, gate=None):
    hidden = weight.shape[0]
    rows = sum(x.size for x in xs) // xs[0].shape[1]
    lane = rows // groups
    operands = list(xs) + [perm, weight]
    specs = [whole()] * (len(xs) + 1) + [in_hbm()]
    aliases = {}
    acc_shape = jax.ShapeDtypeStruct((rows, hidden), jnp.float32)
    if stage != "first":
        aliases = {len(operands): 1 if stage == "last" else 0}
        operands.append(acc)
        specs.append(whole())
    scratch = [
        VMEM((rows, width), jnp.bfloat16),
        VMEM((hidden, width), jnp.bfloat16),
        pltpu.SemaphoreType.DMA((len(cuts) - 1,)),
    ]
    if stage == "dots":
        operands += [saved, back]
        specs += [in_hbm(), whole()]
        scratch += [VMEM((rows, hidden), jnp.bfloat16), pltpu.SemaphoreType.DMA((len(cuts) - 1,))]
        out_shape = [acc_shape] + [jax.ShapeDtypeStruct((lane, 128), jnp.float32)] * groups
        out_specs = [whole()] * len(out_shape)
    elif stage == "last":
        operands.append(gate)
        specs.append(whole())
        out_shape = [jax.ShapeDtypeStruct((rows, hidden), jnp.bfloat16), acc_shape]
        out_specs = [in_hbm(), whole()]
        scratch += [VMEM((rows, hidden), jnp.bfloat16), pltpu.SemaphoreType.DMA((len(cuts) - 1,))]
    elif stage == "first":
        out_shape = [acc_shape, jax.ShapeDtypeStruct((rows, 128), jnp.float32)]
        out_specs = [whole(), whole()]
    else:
        out_shape, out_specs = acc_shape, whole()
    return pl.pallas_call(
        functools.partial(chunk_kernel, stage, len(xs), lane, offset, width, cuts),
        in_specs=specs,
        out_specs=out_specs,
        out_shape=out_shape,
        scratch_shapes=scratch,
        input_output_aliases=aliases,
        compiler_params=pltpu.CompilerParams(vmem_limit_bytes=room(stage, rows, hidden, width, cuts)),
        cost_estimate=cost(2 * rows * hidden * width),
        name="chunk_" + stage,
    )(*operands)


def dots_kernel(experts, rows, groups, *refs):
    x_refs = refs[:experts]
    y_refs = refs[experts : experts + groups]
    early_refs = refs[experts + groups : experts + 2 * groups]
    outs = refs[experts + 2 * groups :]
    for k in range(experts):
        span = slice(k * rows, (k + 1) * rows)
        y = y_refs[0][span, :]
        early = early_refs[0][span, :]
        for other in range(1, groups):
            y = y + y_refs[other][span, :]
            early = early + early_refs[other][span, :]
        late = jnp.sum(x_refs[k][...].astype(jnp.float32) * y, axis=1, keepdims=True)
        outs[k][...] = jnp.transpose(early + late)[0:8]


def late_dots(experts, groups, xs, ys, earlies):
    rows = xs[0].shape[0]
    lane = experts * rows
    return pl.pallas_call(
        functools.partial(dots_kernel, experts, rows, groups),
        in_specs=[whole()] * (experts + 2 * groups),
        out_specs=[whole()] * experts,
        out_shape=[jax.ShapeDtypeStruct((8, rows), jnp.float32)] * experts,
        compiler_params=pltpu.CompilerParams(vmem_limit_bytes=16 * MIB),
        cost_estimate=cost(1),
        name="gate_dots",
    )(*xs, *ys, *earlies)


def plan_kernel(dims, groups, extra_ref, pick_ref, token_ref):
    experts, tok, cap, micro = dims
    total = micro * tok
    small = extra_ref[experts : experts + 4, 0:total]
    picks, names, gates = routing(small, place(experts, groups)[0], experts, tok, cap, micro)
    for k in range(experts):
        both = jnp.concatenate([picks[k] * names[k][0], picks[k] * names[k][1]], axis=1)
        pick_ref[k] = both.astype(jnp.bfloat16)
    lines = list(gates)
    for side in range(2):
        for e in range(experts):
            lines.append((small[side : side + 1] == e).astype(jnp.float32))
    lines.append(jnp.zeros((128 - len(lines), total), jnp.float32))
    token_ref[...] = jnp.transpose(jnp.concatenate(lines, axis=0))


def plan(dims, groups, extra):
    experts, tok, cap, micro = dims
    total = micro * tok
    return pl.pallas_call(
        functools.partial(plan_kernel, dims, groups),
        in_specs=[whole()],
        out_specs=[whole(), whole()],
        out_shape=[
            jax.ShapeDtypeStruct((experts, micro * cap, 2 * total), jnp.bfloat16),
            jax.ShapeDtypeStruct((total, 128), jnp.float32),
        ],
        compiler_params=pltpu.CompilerParams(vmem_limit_bytes=16 * MIB),
        cost_estimate=cost(1),
        name="plan",
    )(extra)


def final_kernel(experts, pick_ref, token_ref, router_ref, dy_ref, *refs):
    dot_refs, out_ref = refs[:experts], refs[experts]
    total = dy_ref.shape[0]
    pair = None
    for k in range(experts):
        line = dot_refs[k][0:1]
        parts = []
        for _ in range(3):
            piece = line.astype(jnp.bfloat16).astype(jnp.float32)
            line = line - piece
            parts.append(piece)
        parts.append(jnp.zeros((5, line.shape[1]), jnp.float32))
        rows = jnp.concatenate(parts, axis=0).astype(jnp.bfloat16)
        term = lax.dot_general(
            pick_ref[k], rows, (((0,), (1,)), ((), ())), preferred_element_type=jnp.float32
        )
        pair = term if pair is None else pair + term
    pair = pair[:, 0:1] + pair[:, 1:2] + pair[:, 2:3]
    pair0, pair1 = pair[0:total], pair[total : 2 * total]
    gate0, gate1 = token_ref[:, 0:1], token_ref[:, 1:2]
    mixed = gate0 * pair0 + gate1 * pair1
    grad0 = gate0 * (pair0 - mixed)
    grad1 = gate1 * (pair1 - mixed)
    spread = []
    for e in range(experts):
        spread.append(
            token_ref[:, 2 + e : 3 + e] * grad0 + token_ref[:, 2 + experts + e : 3 + experts + e] * grad1
        )
    width = 512
    for at in range(0, dy_ref.shape[1], width):
        value = dy_ref[:, at : at + width].astype(jnp.float32)
        term = spread[0] * router_ref[0:1, at : at + width]
        for e in range(1, experts):
            term = term + spread[e] * router_ref[e : e + 1, at : at + width]
        out_ref[:, at : at + width] = (value + term).astype(jnp.bfloat16)


def finish(experts, pick, token, router, dy, dots):
    return pl.pallas_call(
        functools.partial(final_kernel, experts),
        in_specs=[whole()] * (4 + experts),
        out_specs=whole(),
        out_shape=jax.ShapeDtypeStruct(dy.shape, jnp.bfloat16),
        compiler_params=pltpu.CompilerParams(vmem_limit_bytes=16 * MIB),
        cost_estimate=cost(1),
        name="input_grad",
    )(pick, token, router, dy, *dots)


def after(value, *others):
    return lax.optimization_barrier((value,) + others)[0]


def local(upstream_dy, gate_logits, expert_ids, saved_hidden, down_weight, router_weight):
    devices = lax.axis_size("expert")
    sections = lax.axis_size("section")
    _, micro, tok, width = upstream_dy.shape
    experts = router_weight.shape[2]
    cap = saved_hidden.shape[3]
    groups = devices // experts
    hidden = down_weight.shape[1]
    rows = micro * cap
    dims = (experts, tok, cap, micro)

    def to_chip(value, k):
        return lax.ppermute(
            value, "expert", [(i, (i + k * groups) % devices) for i in range(devices)]
        )

    def to_member(value, r):
        return lax.ppermute(
            value,
            "expert",
            [(i, i // groups * groups + (i % groups + r) % groups) for i in range(devices)],
        )

    def to_previous(value):
        return lax.ppermute(value, "section", [(s, s - 1) for s in range(1, sections)])

    def dots_home(value, k):
        pairs = []
        for s in range(1, sections):
            for i in range(devices):
                pairs.append((s * devices + i, (s - 1) * devices + (i + devices - k * groups) % devices))
        return lax.ppermute(value, ("section", "expert"), pairs)

    tokens = micro * tok
    dy = upstream_dy.reshape(tokens, width)
    weight = down_weight[0]
    saved = saved_hidden[0].transpose(0, 2, 1, 3).reshape(-1, hidden)

    part = width // 12
    widths = [3 * part, 4 * part, 3 * part, 2 * part] if devices * rows <= 1024 else [part] * 12
    offsets = [sum(widths[:n]) for n in range(len(widths))]
    count = len(widths)
    first = first_pack(
        dims,
        groups,
        widths[0],
        expert_ids[0].transpose(0, 2, 1),
        gate_logits[0].transpose(0, 2, 1),
        dy,
    )
    small, slot_matrix = first[-2], first[-1]
    rest = rest_pack(experts, rows, offsets[1:], widths[1:], slot_matrix, dy, small, router_weight[0].T)
    sends = [first[:experts]] + [rest[n * experts : (n + 1) * experts] for n in range(count - 1)]

    order = [3, 2, 1] if experts == 4 else list(range(1, experts))

    def travel(n, *others):
        here = [sends[n][0]] + [None] * (experts - 1)
        for k in order:
            value = sends[n][k]
            if n > 0:
                value = after(value, got[n - 1][k], *others)
            here[k] = to_chip(value, k)
        got.append(here)

    def both(here, *others):
        out = [after(piece, *others) for piece in here]
        return here + [to_member(piece, r) for r in range(1, groups) for piece in out]

    got = []
    travel(0)
    travel(1)
    extra_next = to_previous(after(rest[-1], got[0][order[0]]))
    dy_next = to_previous(after(dy, got[0][order[0]]))

    cuts = cut(hidden, (1, 1, 2, 2, 2))
    made = saved_forward(experts, groups, rest[0], saved, weight, offsets[-1], widths[-1], cuts)
    ys, perm, back = made[:groups], made[groups], made[groups + 1]
    ys = [ys[0]] + [to_member(ys[q], -q) for q in range(1, groups)]
    pick, token = plan(dims, groups, extra_next)

    acc = perm
    for n in range(count - 1):
        xs = both(got[n], acc, pick) if n == 1 else both(got[n], acc)
        if n == 0:
            acc, gate = chunk("first", groups, offsets[n], widths[n], cuts, weight, xs, perm)
        elif n < count - 2:
            acc = chunk("middle", groups, offsets[n], widths[n], cuts, weight, xs, perm, acc=acc)
        else:
            acc, *early = chunk(
                "dots", groups, offsets[n], widths[n], cuts, weight, xs, perm, acc=acc, saved=saved, back=back
            )
        if n + 2 < count:
            travel(n + 2, acc)
    earlies = [early[0]] + [to_member(early[q], -q) for q in range(1, groups)]
    xs = both(got[-1], acc)
    dots = late_dots(experts, groups, got[-1], ys, earlies)
    homes = [dots_home(dots[k], k) for k in range(experts)]
    hidden_grad, _ = chunk(
        "last", groups, offsets[-1], widths[-1], cuts, weight, xs, perm, acc=acc, gate=gate
    )
    result = finish(experts, pick, token, extra_next, dy_next, homes)
    hidden_grad = hidden_grad.reshape(micro, cap, devices, hidden).transpose(0, 2, 1, 3)
    return (hidden_grad[None], result.reshape(upstream_dy.shape))


def solution(mesh):
    placed = (
        P("section", None, "expert", None),
        P("section", None, "expert", None),
        P("section", None, "expert", None),
        P("section", None, None, None, "expert"),
        P("section", "expert", None),
        P("section", None, None),
    )
    return jax.shard_map(
        local,
        mesh=mesh,
        in_specs=placed,
        out_specs=(P("section", None, None, None, "expert"), P("section", None, "expert", None)),
        check_vma=False,
    )
```

```python
import functools

import jax
import jax.numpy as jnp
from jax import lax
from jax.experimental import pallas as pl
from jax.experimental.pallas import tpu as pltpu
from jax.sharding import PartitionSpec as P

VMEM = pltpu.VMEM
HIGHEST = lax.Precision.HIGHEST
MIB = 1024 * 1024
SCALE = 0.001


def whole():
    return pl.BlockSpec(memory_space=VMEM)


def in_hbm():
    return pl.BlockSpec(memory_space=pltpu.HBM)


def cost(flops):
    return pl.CostEstimate(flops=max(1, int(SCALE * flops)), bytes_accessed=1, transcendentals=0)


def routing(small, expert0, experts, tok, cap, micro):
    total = small.shape[1]
    id0, id1 = small[0:1], small[1:2]
    gate0 = jax.nn.sigmoid(small[2:3] - small[3:4])
    gate1 = jax.nn.sigmoid(small[3:4] - small[2:3])
    names = []
    for k in range(experts):
        e = lax.rem(expert0 + k, experts).astype(jnp.float32)
        names.append(((id0 == e).astype(jnp.float32), (id1 == e).astype(jnp.float32)))
    hits = jnp.concatenate([a + b for a, b in names] * (8 // experts), axis=0)
    before = lax.broadcasted_iota(jnp.int32, (total, total), 0)
    after = lax.broadcasted_iota(jnp.int32, (total, total), 1)
    same = (before < after) & (before // tok == after // tok)
    ranks = jnp.dot(
        hits.astype(jnp.bfloat16),
        same.astype(jnp.float32).astype(jnp.bfloat16),
        preferred_element_type=jnp.float32,
    )
    row = lax.broadcasted_iota(jnp.int32, (micro * cap, total), 0)
    token = lax.broadcasted_iota(jnp.int32, (micro * cap, total), 1)
    slot = (row % cap).astype(jnp.float32)
    same_micro = row // cap == token // tok
    picks = []
    for k in range(experts):
        mask = (ranks[k : k + 1] == slot) & (hits[k : k + 1] > 0) & same_micro
        picks.append(mask.astype(jnp.float32))
    return picks, names, (gate0, gate1)


def first_pack_kernel(dims, groups, ids_ref, logits_ref, dy_ref, *outs):
    experts, tok, cap, micro = dims
    lines = []
    for ref in (ids_ref, logits_ref):
        for side in range(2):
            parts = [ref[m, side : side + 1, :].astype(jnp.float32) for m in range(micro)]
            lines.append(jnp.concatenate(parts, axis=1))
    small = jnp.concatenate(lines + lines, axis=0)
    picks, names, gates = routing(small, place(experts, groups)[0], experts, tok, cap, micro)
    rows = micro * cap
    flat = jnp.concatenate(picks, axis=0).astype(jnp.bfloat16)
    block = jnp.dot(flat, dy_ref[...], preferred_element_type=jnp.float32)
    width = dy_ref.shape[1]
    for k in range(experts):
        outs[k][:, 0:width] = block[k * rows : (k + 1) * rows].astype(jnp.bfloat16)
        gate = names[k][0] * gates[0] + names[k][1] * gates[1]
        slot_gate = jnp.sum(picks[k] * gate, axis=1, keepdims=True)
        outs[k][:, width:] = jnp.broadcast_to(slot_gate, (rows, 128)).astype(jnp.bfloat16)
    outs[-2][...] = small
    outs[-1][...] = flat


def first_pack(dims, groups, width, ids, logits, dy):
    experts, tok, cap, micro = dims
    rows = micro * cap
    tokens = dy.shape[0]
    shapes = [jax.ShapeDtypeStruct((rows, width + 128), jnp.bfloat16)] * experts
    shapes += [
        jax.ShapeDtypeStruct((8, tokens), jnp.float32),
        jax.ShapeDtypeStruct((experts * rows, tokens), jnp.bfloat16),
    ]
    return pl.pallas_call(
        functools.partial(first_pack_kernel, dims, groups),
        grid=(1,),
        in_specs=[whole(), whole(), pl.BlockSpec((tokens, width), lambda i: (0, 0))],
        out_specs=[whole()] * len(shapes),
        out_shape=shapes,
        compiler_params=pltpu.CompilerParams(vmem_limit_bytes=16 * MIB),
        cost_estimate=cost(1),
        name="pack_first",
    )(ids, logits, dy)


def rest_pack_kernel(experts, rows, offsets, widths, flat_ref, dy_ref, small_ref, router_ref, *outs):
    flat = flat_ref[...]
    outs[-1][0:experts, :] = router_ref[...]
    outs[-1][experts:, :] = jnp.zeros((outs[-1].shape[0] - experts, dy_ref.shape[1]), jnp.float32)
    outs[-1][experts : experts + 4, 0 : small_ref.shape[1]] = small_ref[0:4]
    for n, (offset, width) in enumerate(zip(offsets, widths)):
        block = jnp.dot(flat, dy_ref[:, offset : offset + width], preferred_element_type=jnp.float32)
        for k in range(experts):
            outs[n * experts + k][...] = block[k * rows : (k + 1) * rows].astype(jnp.bfloat16)


def rest_pack(experts, rows, offsets, widths, flat, dy, small, router):
    shapes = [
        jax.ShapeDtypeStruct((rows, width), jnp.bfloat16) for width in widths for _ in range(experts)
    ]
    shapes.append(jax.ShapeDtypeStruct((experts + 4, dy.shape[1]), jnp.float32))
    return pl.pallas_call(
        functools.partial(rest_pack_kernel, experts, rows, offsets, widths),
        in_specs=[whole()] * 4,
        out_specs=[whole()] * len(shapes),
        out_shape=shapes,
        compiler_params=pltpu.CompilerParams(vmem_limit_bytes=24 * MIB),
        cost_estimate=cost(1),
        name="pack_rest",
    )(flat, dy, small, router)


def saved_kernel(experts, groups, lane, offset, cuts, _, saved_ref, w_ref, *refs):
    ys, perm_ref, back_ref = refs[:groups], refs[groups], refs[groups + 1]
    saved_buf, w_buf, saved_sem, w_sem = refs[groups + 2 :]
    spans = list(zip(cuts[:-1], cuts[1:]))
    width = w_buf.shape[1]

    def fetch_saved(i):
        low, high = spans[i]
        return pltpu.make_async_copy(saved_ref.at[:, low:high], saved_buf.at[:, low:high], saved_sem.at[i])

    def fetch_weight(i):
        low, high = spans[i]
        return pltpu.make_async_copy(
            w_ref.at[low:high, offset : offset + width], w_buf.at[low:high, :], w_sem.at[i]
        )

    for i in range(len(spans)):
        fetch_saved(i).start()
        fetch_weight(i).start()

    rows = perm_ref.shape[0]
    sources = experts * groups
    each = rows // sources
    g, c = place(experts, groups)

    def target(dim, shape):
        at = lax.broadcasted_iota(jnp.int32, shape, dim)
        block = at // each
        source = jnp.zeros(shape, jnp.int32)
        for q in range(groups):
            for k in range(experts):
                j = lax.rem(g + experts - k, experts) * groups + lax.rem(c + groups - q, groups)
                source = jnp.where(block == q * experts + k, j, source)
        return (at - block * each) * sources + source

    span = 48 if rows % 48 == 0 else 16
    lanes = target(1, (1, rows))
    plain = lax.broadcasted_iota(jnp.int32, (span, rows), 1)
    for s in range(rows // span):
        at = lax.broadcasted_iota(jnp.int32, (span, rows), 0) + s * span
        perm_ref[s * span : (s + 1) * span, :] = (at == lanes).astype(jnp.float32).astype(jnp.bfloat16)
    column = target(0, (rows, 128))
    for s in range(rows // span):
        there = column[s * span : (s + 1) * span, 0:1]
        back_ref[s * span : (s + 1) * span, :] = (plain == there).astype(jnp.float32).astype(jnp.bfloat16)

    total = None
    for i, (low, high) in enumerate(spans):
        fetch_saved(i).wait()
        fetch_weight(i).wait()
        part = jnp.dot(saved_buf[:, low:high], w_buf[low:high, :], preferred_element_type=jnp.float32)
        total = part if total is None else total + part
    ordered = exact_rows(back_ref[...], total, 2)
    for q in range(groups):
        ys[q][...] = ordered[q * lane : (q + 1) * lane]


def place(experts, groups):
    index = lax.axis_index("expert")
    return index // groups, index % groups


def exact_rows(matrix, value, parts):
    total = None
    for _ in range(parts):
        piece = value.astype(jnp.bfloat16)
        value = value - piece.astype(jnp.float32)
        term = jnp.dot(matrix, piece, preferred_element_type=jnp.float32)
        total = term if total is None else total + term
    return total


def saved_forward(experts, groups, first, saved, weight, offset, width, cuts):
    rows, hidden = saved.shape
    lane = rows // groups
    shapes = [jax.ShapeDtypeStruct((lane, width), jnp.float32)] * groups
    shapes += [jax.ShapeDtypeStruct((rows, rows), jnp.bfloat16)] * 2
    return pl.pallas_call(
        functools.partial(saved_kernel, experts, groups, lane, offset, cuts),
        in_specs=[in_hbm()] * 3,
        out_specs=[whole()] * len(shapes),
        out_shape=shapes,
        scratch_shapes=[
            VMEM((rows, hidden), jnp.bfloat16),
            VMEM((hidden, width), jnp.bfloat16),
            pltpu.SemaphoreType.DMA((len(cuts) - 1,)),
            pltpu.SemaphoreType.DMA((len(cuts) - 1,)),
        ],
        compiler_params=pltpu.CompilerParams(vmem_limit_bytes=(119 if rows <= 1024 else 125) * (MIB // 2) - 4 * lane * groups * width - 4 * rows * rows),
        cost_estimate=cost(2 * rows * hidden * width),
        name="saved_times_weight",
    )(first, saved, weight)


def chunk_kernel(stage, pieces, lane, offset, width, cuts, *refs):
    refs = list(refs)
    x_refs = [refs.pop(0) for _ in range(pieces)]
    perm_ref, w_ref = refs.pop(0), refs.pop(0)
    if stage == "last":
        acc_in, gate_ref, out_ref, _, x_all, w_buf, w_sem, out_buf, out_sem = refs
    elif stage == "dots":
        acc_in, saved_ref, back_ref, acc_ref = refs[:4]
        early_refs, (x_all, w_buf, w_sem, saved_buf, saved_sem) = refs[4:-5], refs[-5:]
    elif stage == "middle":
        acc_in, acc_ref, x_all, w_buf, w_sem = refs
    else:
        acc_ref, gate_ref, x_all, w_buf, w_sem = refs
    spans = list(zip(cuts[:-1], cuts[1:]))

    def fetch(i):
        low, high = spans[i]
        return pltpu.make_async_copy(
            w_ref.at[low:high, offset : offset + width], w_buf.at[low:high, :], w_sem.at[i]
        )

    def send(i):
        low, high = spans[i]
        return pltpu.make_async_copy(out_buf.at[:, low:high], out_ref.at[:, low:high], out_sem.at[i])

    def fetch_saved(i):
        low, high = spans[i]
        return pltpu.make_async_copy(saved_ref.at[:, low:high], saved_buf.at[:, low:high], saved_sem.at[i])

    for i in range(len(spans)):
        fetch(i).start()
        if stage == "dots":
            fetch_saved(i).start()
    values = [r[...].astype(jnp.float32) for r in x_refs]
    mixed = jnp.concatenate(values, axis=0).astype(jnp.bfloat16)
    mixed = jnp.dot(perm_ref[...], mixed, preferred_element_type=jnp.float32)
    x_all[...] = mixed[:, 0:width].astype(jnp.bfloat16)
    if stage == "first":
        gate_ref[...] = mixed[:, width:]
    if stage == "last":
        gate = gate_ref[:, 0:1]
    dots = None
    for i, (low, high) in enumerate(spans):
        fetch(i).wait()
        raw = lax.dot_general(
            x_all[...], w_buf[low:high, :], (((1,), (1,)), ((), ())), preferred_element_type=jnp.float32
        )
        if stage != "first":
            raw = acc_in[:, low:high] + raw
        if stage == "last":
            out_buf[:, low:high] = (raw * gate).astype(jnp.bfloat16)
            send(i).start()
        else:
            acc_ref[:, low:high] = raw
        if stage == "dots":
            fetch_saved(i).wait()
            product = raw * saved_buf[:, low:high].astype(jnp.float32)
            for at in range(0, high - low, 128):
                piece = product[:, at : at + 128]
                dots = piece if dots is None else dots + piece
    if stage == "dots":
        total = jnp.sum(dots, axis=1, keepdims=True)
        ordered = exact_rows(back_ref[...], jnp.broadcast_to(total, dots.shape), 3)
        for q, ref in enumerate(early_refs):
            ref[...] = ordered[q * lane : (q + 1) * lane]
    if stage == "last":
        for i in range(len(spans)):
            send(i).wait()


def cut(total, parts):
    points = [0]
    for part in parts:
        points.append(points[-1] + total * part // sum(parts))
    return points


def room(stage, rows, hidden, width, cuts):
    span = max(b - a for a, b in zip(cuts[:-1], cuts[1:]))
    each = 8 if rows <= 1024 else 14
    total = hidden * width * 2 + rows * width * each + rows * span * 8 + 3 * MIB
    if stage in ("dots", "last"):
        total += rows * hidden * 2
    if stage == "dots":
        total += rows * 128 * 24
    return total


def chunk(stage, groups, offset, width, cuts, weight, xs, perm, acc=None, saved=None, back=None, gate=None):
    hidden = weight.shape[0]
    rows = sum(x.size for x in xs) // xs[0].shape[1]
    lane = rows // groups
    operands = list(xs) + [perm, weight]
    specs = [whole()] * (len(xs) + 1) + [in_hbm()]
    aliases = {}
    acc_shape = jax.ShapeDtypeStruct((rows, hidden), jnp.float32)
    if stage != "first":
        aliases = {len(operands): 1 if stage == "last" else 0}
        operands.append(acc)
        specs.append(whole())
    scratch = [
        VMEM((rows, width), jnp.bfloat16),
        VMEM((hidden, width), jnp.bfloat16),
        pltpu.SemaphoreType.DMA((len(cuts) - 1,)),
    ]
    if stage == "dots":
        operands += [saved, back]
        specs += [in_hbm(), whole()]
        scratch += [VMEM((rows, hidden), jnp.bfloat16), pltpu.SemaphoreType.DMA((len(cuts) - 1,))]
        out_shape = [acc_shape] + [jax.ShapeDtypeStruct((lane, 128), jnp.float32)] * groups
        out_specs = [whole()] * len(out_shape)
    elif stage == "last":
        operands.append(gate)
        specs.append(whole())
        out_shape = [jax.ShapeDtypeStruct((rows, hidden), jnp.bfloat16), acc_shape]
        out_specs = [in_hbm(), whole()]
        scratch += [VMEM((rows, hidden), jnp.bfloat16), pltpu.SemaphoreType.DMA((len(cuts) - 1,))]
    elif stage == "first":
        out_shape = [acc_shape, jax.ShapeDtypeStruct((rows, 128), jnp.float32)]
        out_specs = [whole(), whole()]
    else:
        out_shape, out_specs = acc_shape, whole()
    return pl.pallas_call(
        functools.partial(chunk_kernel, stage, len(xs), lane, offset, width, cuts),
        in_specs=specs,
        out_specs=out_specs,
        out_shape=out_shape,
        scratch_shapes=scratch,
        input_output_aliases=aliases,
        compiler_params=pltpu.CompilerParams(vmem_limit_bytes=room(stage, rows, hidden, width, cuts)),
        cost_estimate=cost(2 * rows * hidden * width),
        name="chunk_" + stage,
    )(*operands)


def dots_kernel(experts, rows, groups, *refs):
    x_refs = refs[:experts]
    y_refs = refs[experts : experts + groups]
    early_refs = refs[experts + groups : experts + 2 * groups]
    (out_ref,) = refs[experts + 2 * groups :]
    lines = []
    for k in range(experts):
        span = slice(k * rows, (k + 1) * rows)
        y = y_refs[0][span, :]
        early = early_refs[0][span, :]
        for other in range(1, groups):
            y = y + y_refs[other][span, :]
            early = early + early_refs[other][span, :]
        late = jnp.sum(x_refs[k][...].astype(jnp.float32) * y, axis=1, keepdims=True)
        lines.append(jnp.transpose(early + late)[0:1])
    out_ref[...] = jnp.concatenate(lines * (8 // experts), axis=0)


def late_dots(experts, groups, xs, ys, earlies):
    rows = xs[0].shape[0]
    lane = experts * rows
    return pl.pallas_call(
        functools.partial(dots_kernel, experts, rows, groups),
        in_specs=[whole()] * (experts + 2 * groups),
        out_specs=whole(),
        out_shape=jax.ShapeDtypeStruct((8, rows), jnp.float32),
        compiler_params=pltpu.CompilerParams(vmem_limit_bytes=16 * MIB),
        cost_estimate=cost(1),
        name="gate_dots",
    )(*xs, *ys, *earlies)


def plan_kernel(dims, groups, extra_ref, pick_ref, token_ref):
    experts, tok, cap, micro = dims
    total = micro * tok
    small = extra_ref[experts : experts + 4, 0:total]
    picks, names, gates = routing(small, place(experts, groups)[0], experts, tok, cap, micro)
    for k in range(experts):
        both = jnp.concatenate([picks[k] * names[k][0], picks[k] * names[k][1]], axis=1)
        pick_ref[k] = both.astype(jnp.bfloat16)
    lines = list(gates)
    for side in range(2):
        for e in range(experts):
            lines.append((small[side : side + 1] == e).astype(jnp.float32))
    lines.append(jnp.zeros((128 - len(lines), total), jnp.float32))
    token_ref[...] = jnp.transpose(jnp.concatenate(lines, axis=0))


def plan(dims, groups, extra):
    experts, tok, cap, micro = dims
    total = micro * tok
    return pl.pallas_call(
        functools.partial(plan_kernel, dims, groups),
        in_specs=[whole()],
        out_specs=[whole(), whole()],
        out_shape=[
            jax.ShapeDtypeStruct((experts, micro * cap, 2 * total), jnp.bfloat16),
            jax.ShapeDtypeStruct((total, 128), jnp.float32),
        ],
        compiler_params=pltpu.CompilerParams(vmem_limit_bytes=16 * MIB),
        cost_estimate=cost(1),
        name="plan",
    )(extra)


def final_kernel(experts, pick_ref, token_ref, router_ref, dy_ref, *refs):
    dot_refs, out_ref = refs[:experts], refs[experts]
    total = dy_ref.shape[0]
    pair = None
    for k in range(experts):
        line = dot_refs[k][k : k + 1]
        parts = []
        for _ in range(3):
            piece = line.astype(jnp.bfloat16).astype(jnp.float32)
            line = line - piece
            parts.append(piece)
        parts.append(jnp.zeros((5, line.shape[1]), jnp.float32))
        rows = jnp.concatenate(parts, axis=0).astype(jnp.bfloat16)
        term = lax.dot_general(
            pick_ref[k], rows, (((0,), (1,)), ((), ())), preferred_element_type=jnp.float32
        )
        pair = term if pair is None else pair + term
    pair = pair[:, 0:1] + pair[:, 1:2] + pair[:, 2:3]
    pair0, pair1 = pair[0:total], pair[total : 2 * total]
    gate0, gate1 = token_ref[:, 0:1], token_ref[:, 1:2]
    mixed = gate0 * pair0 + gate1 * pair1
    grad0 = gate0 * (pair0 - mixed)
    grad1 = gate1 * (pair1 - mixed)
    spread = []
    for e in range(experts):
        spread.append(
            token_ref[:, 2 + e : 3 + e] * grad0 + token_ref[:, 2 + experts + e : 3 + experts + e] * grad1
        )
    width = 512
    for at in range(0, dy_ref.shape[1], width):
        value = dy_ref[:, at : at + width].astype(jnp.float32)
        term = spread[0] * router_ref[0:1, at : at + width]
        for e in range(1, experts):
            term = term + spread[e] * router_ref[e : e + 1, at : at + width]
        out_ref[:, at : at + width] = (value + term).astype(jnp.bfloat16)


def finish(experts, pick, token, router, dy, dots):
    return pl.pallas_call(
        functools.partial(final_kernel, experts),
        in_specs=[whole()] * (4 + experts),
        out_specs=whole(),
        out_shape=jax.ShapeDtypeStruct(dy.shape, jnp.bfloat16),
        compiler_params=pltpu.CompilerParams(vmem_limit_bytes=16 * MIB),
        cost_estimate=cost(1),
        name="input_grad",
    )(pick, token, router, dy, *dots)


def after(value, *others):
    return lax.optimization_barrier((value,) + others)[0]


def local(upstream_dy, gate_logits, expert_ids, saved_hidden, down_weight, router_weight):
    devices = lax.axis_size("expert")
    sections = lax.axis_size("section")
    _, micro, tok, width = upstream_dy.shape
    experts = router_weight.shape[2]
    cap = saved_hidden.shape[3]
    groups = devices // experts
    hidden = down_weight.shape[1]
    rows = micro * cap
    dims = (experts, tok, cap, micro)

    def to_chip(value, k):
        return lax.ppermute(
            value, "expert", [(i, (i + k * groups) % devices) for i in range(devices)]
        )

    def to_member(value, r):
        return lax.ppermute(
            value,
            "expert",
            [(i, i // groups * groups + (i % groups + r) % groups) for i in range(devices)],
        )

    def to_previous(value):
        return lax.ppermute(value, "section", [(s, s - 1) for s in range(1, sections)])

    tokens = micro * tok
    dy = upstream_dy.reshape(tokens, width)
    weight = down_weight[0]
    saved = saved_hidden[0].transpose(0, 2, 1, 3).reshape(-1, hidden)

    part = width // 12
    widths = [3 * part, 4 * part, 3 * part, 2 * part] if devices * rows <= 1024 else [part] * 12
    offsets = [sum(widths[:n]) for n in range(len(widths))]
    count = len(widths)
    first = first_pack(
        dims,
        groups,
        widths[0],
        expert_ids[0].transpose(0, 2, 1),
        gate_logits[0].transpose(0, 2, 1),
        dy,
    )
    small, slot_matrix = first[-2], first[-1]
    rest = rest_pack(experts, rows, offsets[1:], widths[1:], slot_matrix, dy, small, router_weight[0].T)
    sends = [first[:experts]] + [rest[n * experts : (n + 1) * experts] for n in range(count - 1)]

    order = [3, 2, 1] if experts == 4 else list(range(1, experts))

    def travel(n, *others):
        here = [sends[n][0]] + [None] * (experts - 1)
        for k in order:
            value = sends[n][k]
            if n > 0:
                value = after(value, got[n - 1][k], *others)
            here[k] = to_chip(value, k)
        got.append(here)

    def both(here, *others):
        out = [after(piece, *others) for piece in here]
        return here + [to_member(piece, r) for r in range(1, groups) for piece in out]

    got = []
    travel(0)
    travel(1)
    extra_next = to_previous(after(rest[-1], got[0][order[0]]))
    dy_next = to_previous(after(dy, got[0][order[0]]))

    cuts = cut(hidden, (1, 1, 2, 2, 2))
    made = saved_forward(experts, groups, rest[0], saved, weight, offsets[-1], widths[-1], cuts)
    ys, perm, back = made[:groups], made[groups], made[groups + 1]
    ys = [ys[0]] + [to_member(ys[q], -q) for q in range(1, groups)]
    pick, token = plan(dims, groups, extra_next)

    acc = perm
    for n in range(count - 1):
        xs = both(got[n], acc, pick) if n == 1 else both(got[n], acc)
        if n == 0:
            acc, gate = chunk("first", groups, offsets[n], widths[n], cuts, weight, xs, perm)
        elif n < count - 2:
            acc = chunk("middle", groups, offsets[n], widths[n], cuts, weight, xs, perm, acc=acc)
        else:
            acc, *early = chunk(
                "dots", groups, offsets[n], widths[n], cuts, weight, xs, perm, acc=acc, saved=saved, back=back
            )
        if n + 2 < count:
            travel(n + 2, acc)
    earlies = [early[0]] + [to_member(early[q], -q) for q in range(1, groups)]
    xs = both(got[-1], acc)
    dots = late_dots(experts, groups, got[-1], ys, earlies)
    home = to_previous(dots)
    homes = [home] + [to_chip(home, -k) for k in range(1, experts)]
    hidden_grad, _ = chunk(
        "last", groups, offsets[-1], widths[-1], cuts, weight, xs, perm, acc=acc, gate=gate
    )
    result = finish(experts, pick, token, extra_next, dy_next, homes)
    hidden_grad = hidden_grad.reshape(micro, cap, devices, hidden).transpose(0, 2, 1, 3)
    return (hidden_grad[None], result.reshape(upstream_dy.shape))


def solution(mesh):
    placed = (
        P("section", None, "expert", None),
        P("section", None, "expert", None),
        P("section", None, "expert", None),
        P("section", None, None, None, "expert"),
        P("section", "expert", None),
        P("section", None, None),
    )
    return jax.shard_map(
        local,
        mesh=mesh,
        in_specs=placed,
        out_specs=(P("section", None, None, None, "expert"), P("section", None, "expert", None)),
        check_vma=False,
    )
```

```python
import functools

import jax
import jax.numpy as jnp
from jax import lax
from jax.experimental import pallas as pl
from jax.experimental.pallas import tpu as pltpu
from jax.sharding import PartitionSpec as P

VMEM = pltpu.VMEM
HIGHEST = lax.Precision.HIGHEST
MIB = 1024 * 1024
SCALE = 0.001


def whole():
    return pl.BlockSpec(memory_space=VMEM)


def in_hbm():
    return pl.BlockSpec(memory_space=pltpu.HBM)


def cost(flops):
    return pl.CostEstimate(flops=max(1, int(SCALE * flops)), bytes_accessed=1, transcendentals=0)


def routing(small, expert0, experts, tok, cap, micro):
    total = small.shape[1]
    id0, id1 = small[0:1], small[1:2]
    gate0 = jax.nn.sigmoid(small[2:3] - small[3:4])
    gate1 = jax.nn.sigmoid(small[3:4] - small[2:3])
    names = []
    for k in range(experts):
        e = lax.rem(expert0 + k, experts).astype(jnp.float32)
        names.append(((id0 == e).astype(jnp.float32), (id1 == e).astype(jnp.float32)))
    hits = jnp.concatenate([a + b for a, b in names] * (8 // experts), axis=0)
    before = lax.broadcasted_iota(jnp.int32, (total, total), 0)
    after = lax.broadcasted_iota(jnp.int32, (total, total), 1)
    same = (before < after) & (before // tok == after // tok)
    ranks = jnp.dot(
        hits.astype(jnp.bfloat16),
        same.astype(jnp.float32).astype(jnp.bfloat16),
        preferred_element_type=jnp.float32,
    )
    row = lax.broadcasted_iota(jnp.int32, (micro * cap, total), 0)
    token = lax.broadcasted_iota(jnp.int32, (micro * cap, total), 1)
    slot = (row % cap).astype(jnp.float32)
    same_micro = row // cap == token // tok
    picks = []
    for k in range(experts):
        mask = (ranks[k : k + 1] == slot) & (hits[k : k + 1] > 0) & same_micro
        picks.append(mask.astype(jnp.float32))
    return picks, names, (gate0, gate1)


def first_pack_kernel(dims, groups, ids_ref, logits_ref, dy_ref, *outs):
    experts, tok, cap, micro = dims
    lines = []
    for ref in (ids_ref, logits_ref):
        for side in range(2):
            parts = [ref[m, side : side + 1, :].astype(jnp.float32) for m in range(micro)]
            lines.append(jnp.concatenate(parts, axis=1))
    small = jnp.concatenate(lines + lines, axis=0)
    picks, names, gates = routing(small, place(experts, groups)[0], experts, tok, cap, micro)
    rows = micro * cap
    flat = jnp.concatenate(picks, axis=0).astype(jnp.bfloat16)
    block = jnp.dot(flat, dy_ref[...], preferred_element_type=jnp.float32)
    width = dy_ref.shape[1]
    for k in range(experts):
        outs[k][:, 0:width] = block[k * rows : (k + 1) * rows].astype(jnp.bfloat16)
        gate = names[k][0] * gates[0] + names[k][1] * gates[1]
        slot_gate = jnp.sum(picks[k] * gate, axis=1, keepdims=True)
        outs[k][:, width:] = jnp.broadcast_to(slot_gate, (rows, 128)).astype(jnp.bfloat16)
    outs[-2][...] = small
    outs[-1][...] = flat


def first_pack(dims, groups, width, ids, logits, dy):
    experts, tok, cap, micro = dims
    rows = micro * cap
    tokens = dy.shape[0]
    shapes = [jax.ShapeDtypeStruct((rows, width + 128), jnp.bfloat16)] * experts
    shapes += [
        jax.ShapeDtypeStruct((8, tokens), jnp.float32),
        jax.ShapeDtypeStruct((experts * rows, tokens), jnp.bfloat16),
    ]
    return pl.pallas_call(
        functools.partial(first_pack_kernel, dims, groups),
        grid=(1,),
        in_specs=[whole(), whole(), pl.BlockSpec((tokens, width), lambda i: (0, 0))],
        out_specs=[whole()] * len(shapes),
        out_shape=shapes,
        compiler_params=pltpu.CompilerParams(vmem_limit_bytes=16 * MIB),
        cost_estimate=cost(1),
        name="pack_first",
    )(ids, logits, dy)


def rest_pack_kernel(experts, rows, offsets, widths, flat_ref, dy_ref, small_ref, router_ref, *outs):
    flat = flat_ref[...]
    outs[-1][0:experts, :] = router_ref[...]
    outs[-1][experts:, :] = jnp.zeros((outs[-1].shape[0] - experts, dy_ref.shape[1]), jnp.float32)
    outs[-1][experts : experts + 4, 0 : small_ref.shape[1]] = small_ref[0:4]
    for n, (offset, width) in enumerate(zip(offsets, widths)):
        block = jnp.dot(flat, dy_ref[:, offset : offset + width], preferred_element_type=jnp.float32)
        for k in range(experts):
            outs[n * experts + k][...] = block[k * rows : (k + 1) * rows].astype(jnp.bfloat16)


def rest_pack(experts, rows, offsets, widths, flat, dy, small, router):
    shapes = [
        jax.ShapeDtypeStruct((rows, width), jnp.bfloat16) for width in widths for _ in range(experts)
    ]
    shapes.append(jax.ShapeDtypeStruct((experts + 4, dy.shape[1]), jnp.float32))
    return pl.pallas_call(
        functools.partial(rest_pack_kernel, experts, rows, offsets, widths),
        in_specs=[whole()] * 4,
        out_specs=[whole()] * len(shapes),
        out_shape=shapes,
        compiler_params=pltpu.CompilerParams(vmem_limit_bytes=24 * MIB),
        cost_estimate=cost(1),
        name="pack_rest",
    )(flat, dy, small, router)


def saved_kernel(experts, groups, lane, offset, cuts, _, saved_ref, w_ref, *refs):
    ys, perm_ref, back_ref = refs[:groups], refs[groups], refs[groups + 1]
    saved_buf, w_buf, saved_sem, w_sem = refs[groups + 2 :]
    spans = list(zip(cuts[:-1], cuts[1:]))
    width = w_buf.shape[1]

    def fetch_saved(i):
        low, high = spans[i]
        return pltpu.make_async_copy(saved_ref.at[:, low:high], saved_buf.at[:, low:high], saved_sem.at[i])

    def fetch_weight(i):
        low, high = spans[i]
        return pltpu.make_async_copy(
            w_ref.at[low:high, offset : offset + width], w_buf.at[low:high, :], w_sem.at[i]
        )

    for i in range(len(spans)):
        fetch_saved(i).start()
        fetch_weight(i).start()

    rows = perm_ref.shape[0]
    sources = experts * groups
    each = rows // sources
    g, c = place(experts, groups)

    def target(dim, shape):
        at = lax.broadcasted_iota(jnp.int32, shape, dim)
        block = at // each
        source = jnp.zeros(shape, jnp.int32)
        for q in range(groups):
            for k in range(experts):
                j = lax.rem(g + experts - k, experts) * groups + lax.rem(c + groups - q, groups)
                source = jnp.where(block == q * experts + k, j, source)
        return (at - block * each) * sources + source

    span = 48 if rows % 48 == 0 else 16
    lanes = target(1, (1, rows))
    plain = lax.broadcasted_iota(jnp.int32, (span, rows), 1)
    for s in range(rows // span):
        at = lax.broadcasted_iota(jnp.int32, (span, rows), 0) + s * span
        perm_ref[s * span : (s + 1) * span, :] = (at == lanes).astype(jnp.float32).astype(jnp.bfloat16)
    column = target(0, (rows, 128))
    for s in range(rows // span):
        there = column[s * span : (s + 1) * span, 0:1]
        back_ref[s * span : (s + 1) * span, :] = (plain == there).astype(jnp.float32).astype(jnp.bfloat16)

    total = None
    for i, (low, high) in enumerate(spans):
        fetch_saved(i).wait()
        fetch_weight(i).wait()
        part = jnp.dot(saved_buf[:, low:high], w_buf[low:high, :], preferred_element_type=jnp.float32)
        total = part if total is None else total + part
    ordered = exact_rows(back_ref[...], total, 2)
    for q in range(groups):
        ys[q][...] = ordered[q * lane : (q + 1) * lane]


def place(experts, groups):
    index = lax.axis_index("expert")
    return index // groups, index % groups


def exact_rows(matrix, value, parts):
    total = None
    for _ in range(parts):
        piece = value.astype(jnp.bfloat16)
        value = value - piece.astype(jnp.float32)
        term = jnp.dot(matrix, piece, preferred_element_type=jnp.float32)
        total = term if total is None else total + term
    return total


def saved_forward(experts, groups, first, saved, weight, offset, width, cuts):
    rows, hidden = saved.shape
    lane = rows // groups
    shapes = [jax.ShapeDtypeStruct((lane, width), jnp.float32)] * groups
    shapes += [jax.ShapeDtypeStruct((rows, rows), jnp.bfloat16)] * 2
    return pl.pallas_call(
        functools.partial(saved_kernel, experts, groups, lane, offset, cuts),
        in_specs=[in_hbm()] * 3,
        out_specs=[whole()] * len(shapes),
        out_shape=shapes,
        scratch_shapes=[
            VMEM((rows, hidden), jnp.bfloat16),
            VMEM((hidden, width), jnp.bfloat16),
            pltpu.SemaphoreType.DMA((len(cuts) - 1,)),
            pltpu.SemaphoreType.DMA((len(cuts) - 1,)),
        ],
        compiler_params=pltpu.CompilerParams(vmem_limit_bytes=(119 if rows <= 1024 else 125) * (MIB // 2) - 4 * lane * groups * width - 4 * rows * rows),
        cost_estimate=cost(2 * rows * hidden * width),
        name="saved_times_weight",
    )(first, saved, weight)


def chunk_kernel(stage, pieces, lane, offset, width, cuts, *refs):
    refs = list(refs)
    x_refs = [refs.pop(0) for _ in range(pieces)]
    perm_ref, w_ref = refs.pop(0), refs.pop(0)
    if stage == "last":
        acc_in, gate_ref, out_ref, _, x_all, w_buf, w_sem, out_buf, out_sem = refs
    elif stage == "dots":
        acc_in, saved_ref, back_ref, acc_ref = refs[:4]
        early_refs, (x_all, w_buf, w_sem, saved_buf, saved_sem) = refs[4:-5], refs[-5:]
    elif stage == "middle":
        acc_in, acc_ref, x_all, w_buf, w_sem = refs
    else:
        acc_ref, gate_ref, x_all, w_buf, w_sem = refs
    spans = list(zip(cuts[:-1], cuts[1:]))

    def fetch(i):
        low, high = spans[i]
        return pltpu.make_async_copy(
            w_ref.at[low:high, offset : offset + width], w_buf.at[low:high, :], w_sem.at[i]
        )

    def send(i):
        low, high = spans[i]
        return pltpu.make_async_copy(out_buf.at[:, low:high], out_ref.at[:, low:high], out_sem.at[i])

    def fetch_saved(i):
        low, high = spans[i]
        return pltpu.make_async_copy(saved_ref.at[:, low:high], saved_buf.at[:, low:high], saved_sem.at[i])

    for i in range(len(spans)):
        fetch(i).start()
        if stage == "dots":
            fetch_saved(i).start()
    values = [r[...].astype(jnp.float32) for r in x_refs]
    mixed = jnp.concatenate(values, axis=0).astype(jnp.bfloat16)
    mixed = jnp.dot(perm_ref[...], mixed, preferred_element_type=jnp.float32)
    x_all[...] = mixed[:, 0:width].astype(jnp.bfloat16)
    if stage == "first":
        gate_ref[...] = mixed[:, width:]
    if stage == "last":
        gate = gate_ref[:, 0:1]
    dots = None
    for i, (low, high) in enumerate(spans):
        fetch(i).wait()
        raw = lax.dot_general(
            x_all[...], w_buf[low:high, :], (((1,), (1,)), ((), ())), preferred_element_type=jnp.float32
        )
        if stage != "first":
            raw = acc_in[:, low:high] + raw
        if stage == "last":
            out_buf[:, low:high] = (raw * gate).astype(jnp.bfloat16)
            send(i).start()
        else:
            acc_ref[:, low:high] = raw
        if stage == "dots":
            fetch_saved(i).wait()
            product = raw * saved_buf[:, low:high].astype(jnp.float32)
            for at in range(0, high - low, 128):
                piece = product[:, at : at + 128]
                dots = piece if dots is None else dots + piece
    if stage == "dots":
        total = jnp.sum(dots, axis=1, keepdims=True)
        ordered = exact_rows(back_ref[...], jnp.broadcast_to(total, dots.shape), 3)
        for q, ref in enumerate(early_refs):
            ref[...] = ordered[q * lane : (q + 1) * lane]
    if stage == "last":
        for i in range(len(spans)):
            send(i).wait()


def cut(total, parts):
    points = [0]
    for part in parts:
        points.append(points[-1] + total * part // sum(parts))
    return points


def room(stage, rows, hidden, width, cuts):
    span = max(b - a for a, b in zip(cuts[:-1], cuts[1:]))
    each = 8 if rows <= 1024 else 14
    total = hidden * width * 2 + rows * width * each + rows * span * 8 + 3 * MIB
    if stage in ("dots", "last"):
        total += rows * hidden * 2
    if stage == "dots":
        total += rows * 128 * 24
    return total


def chunk(stage, groups, offset, width, cuts, weight, xs, perm, acc=None, saved=None, back=None, gate=None):
    hidden = weight.shape[0]
    rows = sum(x.size for x in xs) // xs[0].shape[1]
    lane = rows // groups
    operands = list(xs) + [perm, weight]
    specs = [whole()] * (len(xs) + 1) + [in_hbm()]
    aliases = {}
    acc_shape = jax.ShapeDtypeStruct((rows, hidden), jnp.float32)
    if stage != "first":
        aliases = {len(operands): 1 if stage == "last" else 0}
        operands.append(acc)
        specs.append(whole())
    scratch = [
        VMEM((rows, width), jnp.bfloat16),
        VMEM((hidden, width), jnp.bfloat16),
        pltpu.SemaphoreType.DMA((len(cuts) - 1,)),
    ]
    if stage == "dots":
        operands += [saved, back]
        specs += [in_hbm(), whole()]
        scratch += [VMEM((rows, hidden), jnp.bfloat16), pltpu.SemaphoreType.DMA((len(cuts) - 1,))]
        out_shape = [acc_shape] + [jax.ShapeDtypeStruct((lane, 128), jnp.float32)] * groups
        out_specs = [whole()] * len(out_shape)
    elif stage == "last":
        operands.append(gate)
        specs.append(whole())
        out_shape = [jax.ShapeDtypeStruct((rows, hidden), jnp.bfloat16), acc_shape]
        out_specs = [in_hbm(), whole()]
        scratch += [VMEM((rows, hidden), jnp.bfloat16), pltpu.SemaphoreType.DMA((len(cuts) - 1,))]
    elif stage == "first":
        out_shape = [acc_shape, jax.ShapeDtypeStruct((rows, 128), jnp.float32)]
        out_specs = [whole(), whole()]
    else:
        out_shape, out_specs = acc_shape, whole()
    return pl.pallas_call(
        functools.partial(chunk_kernel, stage, len(xs), lane, offset, width, cuts),
        in_specs=specs,
        out_specs=out_specs,
        out_shape=out_shape,
        scratch_shapes=scratch,
        input_output_aliases=aliases,
        compiler_params=pltpu.CompilerParams(vmem_limit_bytes=room(stage, rows, hidden, width, cuts)),
        cost_estimate=cost(2 * rows * hidden * width),
        name="chunk_" + stage,
    )(*operands)


def dots_kernel(experts, rows, groups, *refs):
    x_refs = refs[:experts]
    y_refs = refs[experts : experts + groups]
    early_refs = refs[experts + groups : experts + 2 * groups]
    (out_ref,) = refs[experts + 2 * groups :]
    lines = []
    for k in range(experts):
        span = slice(k * rows, (k + 1) * rows)
        y = y_refs[0][span, :]
        early = early_refs[0][span, :]
        for other in range(1, groups):
            y = y + y_refs[other][span, :]
            early = early + early_refs[other][span, :]
        late = jnp.sum(x_refs[k][...].astype(jnp.float32) * y, axis=1, keepdims=True)
        lines.append(jnp.transpose(early + late)[0:1])
    out_ref[...] = jnp.concatenate(lines * (8 // experts), axis=0)


def late_dots(experts, groups, xs, ys, earlies):
    rows = xs[0].shape[0]
    lane = experts * rows
    return pl.pallas_call(
        functools.partial(dots_kernel, experts, rows, groups),
        in_specs=[whole()] * (experts + 2 * groups),
        out_specs=whole(),
        out_shape=jax.ShapeDtypeStruct((8, rows), jnp.float32),
        compiler_params=pltpu.CompilerParams(vmem_limit_bytes=16 * MIB),
        cost_estimate=cost(1),
        name="gate_dots",
    )(*xs, *ys, *earlies)


def plan_kernel(dims, groups, extra_ref, pick_ref, token_ref):
    experts, tok, cap, micro = dims
    total = micro * tok
    small = extra_ref[experts : experts + 4, 0:total]
    picks, names, gates = routing(small, place(experts, groups)[0], experts, tok, cap, micro)
    for k in range(experts):
        both = jnp.concatenate([jnp.transpose(picks[k] * names[k][side]) for side in range(2)], axis=0)
        pick_ref[k] = both.astype(jnp.bfloat16)
    lines = list(gates)
    for side in range(2):
        for e in range(experts):
            lines.append((small[side : side + 1] == e).astype(jnp.float32))
    lines.append(jnp.zeros((128 - len(lines), total), jnp.float32))
    token_ref[...] = jnp.transpose(jnp.concatenate(lines, axis=0))


def plan(dims, groups, extra):
    experts, tok, cap, micro = dims
    total = micro * tok
    return pl.pallas_call(
        functools.partial(plan_kernel, dims, groups),
        in_specs=[whole()],
        out_specs=[whole(), whole()],
        out_shape=[
            jax.ShapeDtypeStruct((experts, 2 * total, micro * cap), jnp.bfloat16),
            jax.ShapeDtypeStruct((total, 128), jnp.float32),
        ],
        compiler_params=pltpu.CompilerParams(vmem_limit_bytes=16 * MIB),
        cost_estimate=cost(1),
        name="plan",
    )(extra)


def final_kernel(experts, pick_ref, token_ref, router_ref, dy_ref, *refs):
    dot_refs, (out_ref, out_buf, out_sem) = refs[:experts], refs[experts:]
    total = dy_ref.shape[0]
    pair = None
    for k in range(experts):
        line = dot_refs[k][k : k + 1]
        parts = []
        for _ in range(3):
            piece = line.astype(jnp.bfloat16).astype(jnp.float32)
            line = line - piece
            parts.append(piece)
        parts.append(jnp.zeros((5, line.shape[1]), jnp.float32))
        rows = jnp.concatenate(parts, axis=0).astype(jnp.bfloat16)
        term = lax.dot_general(
            pick_ref[k], rows, (((1,), (1,)), ((), ())), preferred_element_type=jnp.float32
        )
        pair = term if pair is None else pair + term
    pair = pair[:, 0:1] + pair[:, 1:2] + pair[:, 2:3]
    pair0, pair1 = pair[0:total], pair[total : 2 * total]
    gate0, gate1 = token_ref[:, 0:1], token_ref[:, 1:2]
    mixed = gate0 * pair0 + gate1 * pair1
    grad0 = gate0 * (pair0 - mixed)
    grad1 = gate1 * (pair1 - mixed)
    spread = []
    for e in range(experts):
        spread.append(
            token_ref[:, 2 + e : 3 + e] * grad0 + token_ref[:, 2 + experts + e : 3 + experts + e] * grad1
        )
    width = 512
    copies = []
    for at in range(0, dy_ref.shape[1], width):
        value = dy_ref[:, at : at + width].astype(jnp.float32)
        term = spread[0] * router_ref[0:1, at : at + width]
        for e in range(1, experts):
            term = term + spread[e] * router_ref[e : e + 1, at : at + width]
        out_buf[:, at : at + width] = (value + term).astype(jnp.bfloat16)
        if (at + width) % (4 * width) == 0:
            span = slice(at + width - 4 * width, at + width)
            copies.append(
                pltpu.make_async_copy(out_buf.at[:, span], out_ref.at[:, span], out_sem.at[len(copies)])
            )
            copies[-1].start()
    for copy in copies:
        copy.wait()


def finish(experts, pick, token, router, dy, dots):
    return pl.pallas_call(
        functools.partial(final_kernel, experts),
        in_specs=[whole()] * (4 + experts),
        out_specs=in_hbm(),
        out_shape=jax.ShapeDtypeStruct(dy.shape, jnp.bfloat16),
        scratch_shapes=[VMEM(dy.shape, jnp.bfloat16), pltpu.SemaphoreType.DMA((dy.shape[1] // 2048,))],
        compiler_params=pltpu.CompilerParams(vmem_limit_bytes=16 * MIB),
        cost_estimate=cost(1),
        name="input_grad",
    )(pick, token, router, dy, *dots)


def after(value, *others):
    return lax.optimization_barrier((value,) + others)[0]


def local(upstream_dy, gate_logits, expert_ids, saved_hidden, down_weight, router_weight):
    devices = lax.axis_size("expert")
    sections = lax.axis_size("section")
    _, micro, tok, width = upstream_dy.shape
    experts = router_weight.shape[2]
    cap = saved_hidden.shape[3]
    groups = devices // experts
    hidden = down_weight.shape[1]
    rows = micro * cap
    dims = (experts, tok, cap, micro)

    def to_chip(value, k):
        return lax.ppermute(
            value, "expert", [(i, (i + k * groups) % devices) for i in range(devices)]
        )

    def to_member(value, r):
        return lax.ppermute(
            value,
            "expert",
            [(i, i // groups * groups + (i % groups + r) % groups) for i in range(devices)],
        )

    def to_previous(value):
        return lax.ppermute(value, "section", [(s, s - 1) for s in range(1, sections)])

    tokens = micro * tok
    dy = upstream_dy.reshape(tokens, width)
    weight = down_weight[0]
    saved = saved_hidden[0].transpose(0, 2, 1, 3).reshape(-1, hidden)

    part = width // 12
    widths = [3 * part, 4 * part, 3 * part, 2 * part] if devices * rows <= 1024 else [part] * 12
    offsets = [sum(widths[:n]) for n in range(len(widths))]
    count = len(widths)
    first = first_pack(
        dims,
        groups,
        widths[0],
        expert_ids[0].transpose(0, 2, 1),
        gate_logits[0].transpose(0, 2, 1),
        dy,
    )
    small, slot_matrix = first[-2], first[-1]
    rest = rest_pack(experts, rows, offsets[1:], widths[1:], slot_matrix, dy, small, router_weight[0].T)
    sends = [first[:experts]] + [rest[n * experts : (n + 1) * experts] for n in range(count - 1)]

    order = [3, 2, 1] if experts == 4 else list(range(1, experts))

    def travel(n, *others):
        here = [sends[n][0]] + [None] * (experts - 1)
        for k in order:
            value = sends[n][k]
            if n > 0:
                value = after(value, got[n - 1][k], *others)
            here[k] = to_chip(value, k)
        got.append(here)

    def both(here, *others):
        out = [after(piece, *others) for piece in here]
        return here + [to_member(piece, r) for r in range(1, groups) for piece in out]

    got = []
    travel(0)
    travel(1)
    extra_next = to_previous(after(rest[-1], got[0][order[0]]))
    dy_next = to_previous(after(dy, got[0][order[0]]))

    cuts = cut(hidden, (1, 1, 2, 2, 2))
    made = saved_forward(experts, groups, rest[0], saved, weight, offsets[-1], widths[-1], cuts)
    ys, perm, back = made[:groups], made[groups], made[groups + 1]
    ys = [ys[0]] + [to_member(ys[q], -q) for q in range(1, groups)]
    pick, token = plan(dims, groups, extra_next)

    acc = perm
    for n in range(count - 1):
        xs = both(got[n], acc, pick) if n == 1 else both(got[n], acc)
        if n == 0:
            acc, gate = chunk("first", groups, offsets[n], widths[n], cuts, weight, xs, perm)
        elif n < count - 2:
            acc = chunk("middle", groups, offsets[n], widths[n], cuts, weight, xs, perm, acc=acc)
        else:
            acc, *early = chunk(
                "dots", groups, offsets[n], widths[n], cuts, weight, xs, perm, acc=acc, saved=saved, back=back
            )
        if n + 2 < count:
            travel(n + 2, acc)
    earlies = [early[0]] + [to_member(early[q], -q) for q in range(1, groups)]
    xs = both(got[-1], acc)
    dots = late_dots(experts, groups, got[-1], ys, earlies)
    home = to_previous(dots)
    homes = [home] + [to_chip(home, -k) for k in range(1, experts)]
    hidden_grad, _ = chunk(
        "last", groups, offsets[-1], widths[-1], cuts, weight, xs, perm, acc=acc, gate=gate
    )
    result = finish(experts, pick, token, extra_next, dy_next, homes)
    hidden_grad = hidden_grad.reshape(micro, cap, devices, hidden).transpose(0, 2, 1, 3)
    return (hidden_grad[None], result.reshape(upstream_dy.shape))


def solution(mesh):
    placed = (
        P("section", None, "expert", None),
        P("section", None, "expert", None),
        P("section", None, "expert", None),
        P("section", None, None, None, "expert"),
        P("section", "expert", None),
        P("section", None, None),
    )
    return jax.shard_map(
        local,
        mesh=mesh,
        in_specs=placed,
        out_specs=(P("section", None, None, None, "expert"), P("section", None, "expert", None)),
        check_vma=False,
    )
```
